512 devices in a mesh: row: 32 (over z_lo, y, core), col: 16 (over z_hi, x).
Axes of the slice: x: 4, y: 4, z: 16 (z_hi: 4, z_lo: 4; z = z_hi * 4 + z_lo), core: 2. Of those that a mesh axis runs over, the one named last changes fastest.
Arguments:
- pair: bfloat16 [384, 384, 128], P('row', 'col'), may hold values from -6 to 6
- d_out: bfloat16 [384, 384, 128], P('row', 'col'), may hold values from -6 to 6
- w_proj: bfloat16 [128, 256], replicated, may hold values from -0.5 to 0.5
- w_gate: bfloat16 [128, 128], replicated, may hold values from -0.5 to 0.5
- output_weight: bfloat16 [64, 128], replicated, may hold values from -0.75 to 0.75
Outputs:
- d_pair: float32 [384, 384, 128], P('row', 'col')
The draws below stay inside these ranges and needn't reach their ends.
All inputs are finite; a program needn't handle non-finite values.
Results may differ from the reference program's by a relative error of at most 0.0069.
Values may be sent and summed in bfloat16 or wider, within the bound.
A program may use at most 64 MiB of HBM per device.

```python
import jax
import jax.numpy as jnp
from jax import lax

C = 128
H = 64
N = 384


def levels(rng, dims, cuts, smallest, largest):
    def one(position, parts):
        steps = jax.random.uniform(jax.random.fold_in(jax.random.fold_in(rng, 6), position), (parts,), jnp.float32, smallest / len(cuts), largest / len(cuts))
        return jnp.repeat(jnp.exp(steps), dims[position] // parts).reshape((-1,) + (1,) * (len(dims) - position - 1))

    factor_of = one(*cuts[0])
    for cut in cuts[1:]:
        factor_of = factor_of * one(*cut)
    return factor_of


def bell_draw(own_key, dims, scale, reach, pieces=(), dtype=jnp.bfloat16):
    factor_of = levels(own_key, dims, pieces, -0.22, 0.18) if pieces else 1.0
    array = jax.random.normal(own_key, dims, jnp.float32) * scale * factor_of
    return jnp.minimum(jnp.maximum(array, -reach), reach).astype(dtype)


def setup_inputs(seed: int = 0) -> dict:
    key_list = jax.random.split(jax.random.key(seed), 6)
    return {
        "pair": bell_draw(key_list[0], (N, N, C), 1.0, 6.0, ((0, 32), (1, 16))),
        "d_out": bell_draw(key_list[1], (N, N, C), 1.0, 6.0, ((0, 32), (1, 16))),
        "w_proj": bell_draw(key_list[2], (C, 4 * H), C ** -0.5, 0.5),
        "w_gate": bell_draw(key_list[3], (C, C), C ** -0.5, 0.5),
        "output_weight": bell_draw(key_list[4], (H, C), H ** -0.5, 0.75),
    }


EPS = 1e-05

def apply_layer_norm(values, reduce_dim):
    centre = values - lax.optimization_barrier(jnp.mean(values, axis=reduce_dim, keepdims=True))
    inv_std = jax.lax.rsqrt(lax.optimization_barrier(jnp.mean(centre * centre, axis=reduce_dim, keepdims=True)) + EPS)
    return (centre * inv_std, inv_std)

def layer_norm_backward(upstream, normed, inv_std, reduce_dim):
    grad_mean = lax.optimization_barrier(jnp.mean(upstream, axis=reduce_dim, keepdims=True))
    cross_mean = lax.optimization_barrier(jnp.mean(upstream * normed, axis=reduce_dim, keepdims=True))
    return (upstream - grad_mean - normed * cross_mean) * inv_std

def reference(pair, d_out, w_proj, w_gate, output_weight):
    residue_count = pair.shape[0]
    pair_width = pair.shape[2]
    hidden_channels = output_weight.shape[0]
    pair_cell_count = residue_count * residue_count
    zhat, inv_std = apply_layer_norm(pair.astype(jnp.float32).reshape(pair_cell_count, pair_width), 1)
    normed = zhat.astype(jnp.bfloat16)
    projected = jnp.dot(normed, w_proj, preferred_element_type=jnp.float32)
    a_gate = jax.nn.sigmoid(projected[:, :hidden_channels])
    a_value = projected[:, hidden_channels:2 * hidden_channels]
    b_gate = jax.nn.sigmoid(projected[:, 2 * hidden_channels:3 * hidden_channels])
    b_value = projected[:, 3 * hidden_channels:]
    left = (a_gate * a_value).astype(jnp.bfloat16).reshape(residue_count, residue_count, hidden_channels)
    right = (b_gate * b_value).astype(jnp.bfloat16).reshape(residue_count, residue_count, hidden_channels)
    left_f = left.astype(jnp.float32)
    right_f = right.astype(jnp.float32)
    full_input = jnp.einsum('ikh,jkh->ijh', left_f, right_f).reshape(pair_cell_count, hidden_channels)
    standardized_input, input_inverse_std = apply_layer_norm(full_input, 1)
    mixed_product = jnp.dot(standardized_input.astype(jnp.bfloat16), output_weight, preferred_element_type=jnp.float32)
    gate = jax.nn.sigmoid(jnp.dot(normed, w_gate, preferred_element_type=jnp.float32))
    upstream_out = d_out.reshape(pair_cell_count, pair_width).astype(jnp.float32)
    d_gate = (upstream_out * mixed_product * gate * (1.0 - gate)).astype(jnp.bfloat16)
    mixed_gradient = (upstream_out * gate).astype(jnp.bfloat16)
    standardized_gradient = jnp.dot(mixed_gradient, output_weight.T, preferred_element_type=jnp.float32)
    input_gradient = layer_norm_backward(standardized_gradient, standardized_input, input_inverse_std, 1).astype(jnp.bfloat16).reshape(residue_count, residue_count, hidden_channels)
    d_x_f = input_gradient.astype(jnp.float32)
    d_left = jnp.einsum('ijh,jkh->ikh', d_x_f, right_f).reshape(pair_cell_count, hidden_channels)
    d_right = jnp.einsum('ijh,ikh->jkh', d_x_f, left_f).reshape(pair_cell_count, hidden_channels)
    d_projected = jnp.concatenate([d_left * a_value * a_gate * (1.0 - a_gate), d_left * a_gate, d_right * b_value * b_gate * (1.0 - b_gate), d_right * b_gate], axis=1).astype(jnp.bfloat16)
    d_normed = jnp.dot(d_projected, w_proj.T, preferred_element_type=jnp.float32) + jnp.dot(d_gate, w_gate.T, preferred_element_type=jnp.float32)
    d_pair = layer_norm_backward(d_normed, zhat, inv_std, 1)
    return d_pair.reshape(residue_count, residue_count, pair_width)
```

```python
import functools

import jax
import jax.numpy as jnp
from jax import lax
from jax.experimental import pallas as pl
from jax.experimental.pallas import tpu as pltpu
from jax.sharding import PartitionSpec as P

EPS = 1e-05
MESH = pl.DeviceIdType.MESH
F32 = jnp.float32
BF16 = jnp.bfloat16

ROWS = 32
COLS = 16
OWNERS = 4
OWNER_STEP = 10
HALF = 12
TILE_I = 12
LANES = 128


def dot(a, b):
    return lax.dot_general(a, b, (((1,), (0,)), ((), ())), preferred_element_type=F32)


def dot_t(a, b):
    return lax.dot_general(a, b, (((1,), (1,)), ((), ())), preferred_element_type=F32)


def swap_blocks(parts):
    lane = lax.broadcasted_iota(jnp.int32, parts[0].shape, 1)
    low = lane < 64
    even = (lane // 32) % 2 == 0
    p0, p1, p2, p3 = parts
    t0 = jnp.where(low, p0, pltpu.roll(p2, 64, 1))
    t2 = jnp.where(low, pltpu.roll(p0, 64, 1), p2)
    t1 = jnp.where(low, p1, pltpu.roll(p3, 64, 1))
    t3 = jnp.where(low, pltpu.roll(p1, 64, 1), p3)
    u0 = jnp.where(even, t0, pltpu.roll(t1, 32, 1))
    u1 = jnp.where(even, pltpu.roll(t0, 96, 1), t1)
    u2 = jnp.where(even, t2, pltpu.roll(t3, 32, 1))
    u3 = jnp.where(even, pltpu.roll(t2, 96, 1), t3)
    return u0, u1, u2, u3


def body(
    pair_ref, d_out_ref, w_proj_ref, w_gate_ref, ow_ref, out_ref,
    pad_ref, rows8_ref, rows4_ref, xs_ref,
    send_a, recv_a, send_b, recv_b, send_c, recv_c, send_d, recv_d,
    send_e, recv_e, send_f, recv_f, send_g, recv_g, send_h, recv_h,
    send_sem, recv_sem, quad_sem,
):
    r = lax.axis_index("row")
    c = lax.axis_index("col")
    is_owner = r % OWNER_STEP == 0
    barrier = pltpu.get_barrier_semaphore()

    def greet_col(d, carry):
        pl.semaphore_signal(barrier, inc=1, device_id=(r, lax.rem(c + d, COLS)), device_id_type=MESH)
        return carry

    lax.fori_loop(1, COLS, greet_col, 0)

    @pl.when(is_owner)
    def _():
        def greet_row(d, carry):
            pl.semaphore_signal(barrier, inc=1, device_id=(lax.rem(r + d, ROWS), c), device_id_type=MESH)
            return carry

        lax.fori_loop(1, ROWS, greet_row, 0)

    @pl.when(jnp.logical_not(is_owner))
    def _():
        for q in range(OWNERS):
            pl.semaphore_signal(barrier, inc=1, device_id=(q * OWNER_STEP, c), device_id_type=MESH)

    def padded_transpose(ref):
        for i in range(TILE_I):
            cells = ref[i].astype(F32)
            pad_ref[32 * i : 32 * i + HALF, :] = cells[:HALF]
            pad_ref[32 * i + 16 : 32 * i + 16 + HALF, :] = cells[HALF:]
        return pad_ref[...].T

    def all_to_all(phase, send, recv):
        pltpu.make_async_copy(send.at[c], recv.at[c], recv_sem.at[phase]).start()

        def one(d, carry):
            to = lax.rem(c + d, COLS)
            pltpu.make_async_remote_copy(
                src_ref=send.at[to], dst_ref=recv.at[c],
                send_sem=send_sem.at[phase], recv_sem=recv_sem.at[phase],
                device_id=(r, to), device_id_type=MESH,
            ).start()
            return carry

        lax.fori_loop(1, COLS, one, 0)

    def to_owners(phase, send, recv):
        for q in range(OWNERS):
            @pl.when(r == q * OWNER_STEP)
            def _():
                pltpu.make_async_copy(send.at[q], recv.at[r], recv_sem.at[phase]).start()

            @pl.when(r != q * OWNER_STEP)
            def _():
                pltpu.make_async_remote_copy(
                    src_ref=send.at[q], dst_ref=recv.at[r],
                    send_sem=quad_sem.at[phase, q], recv_sem=recv_sem.at[phase],
                    device_id=(q * OWNER_STEP, c), device_id_type=MESH,
                ).start()

    def from_owner(phase, send, recv):
        q = r // OWNER_STEP
        pltpu.make_async_copy(send.at[r], recv.at[q], quad_sem.at[phase, q]).start()

        def one(d, carry):
            to = lax.rem(r + d, ROWS)
            pltpu.make_async_remote_copy(
                src_ref=send.at[to], dst_ref=recv.at[q],
                send_sem=send_sem.at[phase], recv_sem=quad_sem.at[phase, q],
                device_id=(to, c), device_id_type=MESH,
            ).start()
            return carry

        lax.fori_loop(1, ROWS, one, 0)

    def wait_all(ref, sem):
        pltpu.make_async_copy(ref, ref, sem).wait()

    def wait_quads(phase, recv):
        for q in range(OWNERS):
            wait_all(recv.at[q], quad_sem.at[phase, q])

    def spread(recv, stage, rows):
        for z in range(4):
            for a in range(3):
                parts = [recv[4 * z + x, :, LANES * a : LANES * (a + 1)].astype(F32) for x in range(4)]
                for b, part in enumerate(swap_blocks(parts)):
                    stage[z, pl.ds(4 * a + b, rows, stride=16), :] = part

    def collect(stage, send, rows):
        for z in range(4):
            for a in range(3):
                parts = [stage[z, pl.ds(4 * a + b, rows, stride=16), :] for b in range(4)]
                for x, part in enumerate(swap_blocks(parts)):
                    send[4 * z + x, :, LANES * a : LANES * (a + 1)] = part.astype(BF16)

    pad_ref[...] = jnp.zeros_like(pad_ref)
    rows8_ref[...] = jnp.zeros_like(rows8_ref)
    rows4_ref[...] = jnp.zeros_like(rows4_ref)
    new = lax.broadcasted_iota(jnp.int32, (256, 256), 0)
    old = lax.broadcasted_iota(jnp.int32, (256, 256), 1)
    left_right = new % 2
    q_of = (new // 2) % 4
    col_of = (new // 8) % 16
    value = new // 128
    order = (old == left_right * 128 + value * 64 + col_of * 4 + q_of).astype(F32).astype(BF16)
    w_rows = dot_t(order, w_proj_ref[...]).astype(BF16)
    w_cols = dot_t(w_proj_ref[...], order).astype(BF16)
    eye = (
        lax.broadcasted_iota(jnp.int32, (128, 128), 0) == lax.broadcasted_iota(jnp.int32, (128, 128), 1)
    ).astype(F32).astype(BF16)
    w_gate_t = dot_t(eye, w_gate_ref[...]).astype(BF16)
    ow_t = dot_t(eye, ow_ref[...]).astype(BF16)

    values = padded_transpose(pair_ref)
    centre = values - jnp.mean(values, axis=0, keepdims=True)
    inv_std = lax.rsqrt(jnp.mean(centre * centre, axis=0, keepdims=True) + EPS)
    zhat = centre * inv_std
    normed = zhat.astype(BF16)
    projected = dot(w_rows, normed)
    gates = jax.nn.sigmoid(projected[:128])
    vals = projected[128:]
    send_a[...] = (gates * vals).astype(BF16).reshape(COLS, 8, 384)

    pl.semaphore_wait(barrier, COLS - 1 + jnp.where(is_owner, ROWS - 1, OWNERS))
    all_to_all(0, send_a, recv_a)

    upstream = padded_transpose(d_out_ref)
    gate = jax.nn.sigmoid(dot(w_gate_t, normed))
    d_xhat = dot(ow_ref[...], (upstream * gate).astype(BF16))
    d_xhat_mean = jnp.mean(d_xhat, axis=0, keepdims=True)
    gate_slope = upstream * gate * (1.0 - gate)

    wait_all(recv_a, recv_sem.at[0])
    spread(recv_a, rows8_ref, 8)
    for q in range(OWNERS):
        send_b[q] = rows8_ref[:, 32 * q : 32 * q + 32, :].astype(BF16)
    to_owners(1, send_b, recv_b)

    def matrix(recv, lo):
        return jnp.concatenate(
            [recv[:, z, lo : lo + 16, :].reshape(ROWS * 16, LANES) for z in range(4)], axis=1
        )

    def put(send, lo, product):
        for z in range(4):
            send[:, z, lo : lo + 16, :] = (
                product[:, LANES * z : LANES * (z + 1)].astype(BF16).reshape(ROWS, 16, LANES)
            )

    @pl.when(is_owner)
    def _():
        wait_all(recv_b, recv_sem.at[1])
        put(send_c, 0, dot_t(matrix(recv_b, 0), matrix(recv_b, 16)))
        from_owner(2, send_c, recv_c)

    wait_quads(2, recv_c)
    for z in range(4):
        rows4_ref[z] = recv_c[:, z].reshape(OWNERS * 16, LANES).astype(F32)
    collect(rows4_ref, send_d, 4)
    all_to_all(3, send_d, recv_d)
    wait_all(recv_d, recv_sem.at[3])
    for s in range(COLS):
        xs_ref[4 * s : 4 * s + 4, :] = recv_d[s].astype(F32)

    x = xs_ref[...]
    x_centre = x - jnp.mean(x, axis=0, keepdims=True)
    x_inv = lax.rsqrt(jnp.mean(x_centre * x_centre, axis=0, keepdims=True) + EPS)
    xhat = x_centre * x_inv
    d_x = (d_xhat - d_xhat_mean - xhat * jnp.mean(d_xhat * xhat, axis=0, keepdims=True)) * x_inv
    xs_ref[...] = d_x
    for s in range(COLS):
        send_e[s] = xs_ref[4 * s : 4 * s + 4, :].astype(BF16)
    all_to_all(4, send_e, recv_e)

    mixed = dot(ow_t, xhat.astype(BF16))
    d_gate = (mixed * gate_slope).astype(BF16)
    d_normed_gate = dot(w_gate_ref[...], d_gate)

    wait_all(recv_e, recv_sem.at[4])
    rows4_ref[...] = jnp.zeros_like(rows4_ref)
    spread(recv_e, rows4_ref, 4)
    for q in range(OWNERS):
        send_f[q] = rows4_ref[:, 16 * q : 16 * q + 16, :].astype(BF16)
    to_owners(5, send_f, recv_f)

    @pl.when(is_owner)
    def _():
        wait_all(recv_f, recv_sem.at[5])
        d_x_all = matrix(recv_f, 0)
        put(send_g, 0, dot(d_x_all, matrix(recv_b, 16)))
        put(send_g, 16, dot(d_x_all.astype(F32).T.astype(BF16), matrix(recv_b, 0)))
        from_owner(6, send_g, recv_g)

    wait_quads(6, recv_g)
    for z in range(4):
        rows8_ref[z] = recv_g[:, z].reshape(OWNERS * 32, LANES).astype(F32)
    collect(rows8_ref, send_h, 8)
    all_to_all(7, send_h, recv_h)
    wait_all(recv_h, recv_sem.at[7])

    d_lr = recv_h[...].astype(F32).reshape(COLS * 8, 384)
    d_vals = d_lr * gates
    d_gates = d_vals * vals * (1.0 - gates)
    d_projected = jnp.concatenate([d_gates.astype(BF16), d_vals.astype(BF16)], axis=0)
    d_normed = dot(w_cols, d_projected) + d_normed_gate
    grad_mean = jnp.mean(d_normed, axis=0, keepdims=True)
    cross_mean = jnp.mean(d_normed * zhat, axis=0, keepdims=True)
    pad_ref[...] = ((d_normed - grad_mean - zhat * cross_mean) * inv_std).T
    for i in range(TILE_I):
        out_ref[i, :HALF, :] = pad_ref[32 * i : 32 * i + HALF, :]
        out_ref[i, HALF:, :] = pad_ref[32 * i + 16 : 32 * i + 16 + HALF, :]

    for phase, send in ((0, send_a), (3, send_d), (4, send_e), (7, send_h)):
        wait_all(send.at[pl.ds(0, COLS - 1)], send_sem.at[phase])
    for phase, send in ((1, send_b), (5, send_f)):
        for q in range(OWNERS):
            @pl.when(r != q * OWNER_STEP)
            def _():
                wait_all(send.at[q], quad_sem.at[phase, q])

    @pl.when(is_owner)
    def _():
        for phase, send in ((2, send_c), (6, send_g)):
            wait_all(send.at[pl.ds(0, ROWS - 1)], send_sem.at[phase])


def per_device(pair, d_out, w_proj, w_gate, output_weight):
    vmem = pl.BlockSpec(memory_space=pltpu.VMEM)
    return pl.pallas_call(
        body,
        out_shape=jax.ShapeDtypeStruct(pair.shape, F32),
        in_specs=[vmem] * 5,
        out_specs=vmem,
        scratch_shapes=[
            pltpu.VMEM((384, LANES), F32),
            pltpu.VMEM((4, 128, LANES), F32),
            pltpu.VMEM((4, 64, LANES), F32),
            pltpu.VMEM((64, 384), F32),
            pltpu.VMEM((COLS, 8, 384), BF16),
            pltpu.VMEM((COLS, 8, 384), BF16),
            pltpu.VMEM((OWNERS, 4, 32, LANES), BF16),
            pltpu.VMEM((ROWS, 4, 32, LANES), BF16),
            pltpu.VMEM((ROWS, 4, 16, LANES), BF16),
            pltpu.VMEM((OWNERS, 4, 16, LANES), BF16),
            pltpu.VMEM((COLS, 4, 384), BF16),
            pltpu.VMEM((COLS, 4, 384), BF16),
            pltpu.VMEM((COLS, 4, 384), BF16),
            pltpu.VMEM((COLS, 4, 384), BF16),
            pltpu.VMEM((OWNERS, 4, 16, LANES), BF16),
            pltpu.VMEM((ROWS, 4, 16, LANES), BF16),
            pltpu.VMEM((ROWS, 4, 32, LANES), BF16),
            pltpu.VMEM((OWNERS, 4, 32, LANES), BF16),
            pltpu.VMEM((COLS, 8, 384), BF16),
            pltpu.VMEM((COLS, 8, 384), BF16),
            pltpu.SemaphoreType.DMA((8,)),
            pltpu.SemaphoreType.DMA((8,)),
            pltpu.SemaphoreType.DMA((8, OWNERS)),
        ],
        compiler_params=pltpu.CompilerParams(
            collective_id=0, has_side_effects=True, vmem_limit_bytes=48 * 1024 * 1024
        ),
    )(pair, d_out, w_proj, w_gate, output_weight)


def solution(mesh):
    return jax.shard_map(
        per_device,
        mesh=mesh,
        in_specs=(P("row", "col", None), P("row", "col", None), P(), P(), P()),
        out_specs=P("row", "col", None),
        check_vma=False,
    )
```

```python
import functools

import jax
import jax.numpy as jnp
from jax import lax
from jax.experimental import pallas as pl
from jax.experimental.pallas import tpu as pltpu
from jax.sharding import PartitionSpec as P

EPS = 1e-05
MESH = pl.DeviceIdType.MESH
F32 = jnp.float32
BF16 = jnp.bfloat16

ROWS = 32
COLS = 16
OWNERS = 4
BLOCK = 8
HALF = 12
TILE_I = 12
LANES = 128


def dot(a, b):
    return lax.dot_general(a, b, (((1,), (0,)), ((), ())), preferred_element_type=F32)


def dot_t(a, b):
    return lax.dot_general(a, b, (((1,), (1,)), ((), ())), preferred_element_type=F32)


def swap_blocks(parts):
    lane = lax.broadcasted_iota(jnp.int32, parts[0].shape, 1)
    low = lane < 64
    even = (lane // 32) % 2 == 0
    p0, p1, p2, p3 = parts
    t0 = jnp.where(low, p0, pltpu.roll(p2, 64, 1))
    t2 = jnp.where(low, pltpu.roll(p0, 64, 1), p2)
    t1 = jnp.where(low, p1, pltpu.roll(p3, 64, 1))
    t3 = jnp.where(low, pltpu.roll(p1, 64, 1), p3)
    u0 = jnp.where(even, t0, pltpu.roll(t1, 32, 1))
    u1 = jnp.where(even, pltpu.roll(t0, 96, 1), t1)
    u2 = jnp.where(even, t2, pltpu.roll(t3, 32, 1))
    u3 = jnp.where(even, pltpu.roll(t2, 96, 1), t3)
    return u0, u1, u2, u3


def close_gaps(tiles):
    place = lax.broadcasted_iota(jnp.int32, tiles[0].shape, 1) % 16
    return [
        jnp.where(place < HALF, tiles[t], pltpu.roll(tiles[3], HALF - 4 * t, 1)) for t in range(3)
    ]


def open_gaps(tiles):
    place = lax.broadcasted_iota(jnp.int32, tiles[0].shape, 1) % 16
    back = [pltpu.roll(tiles[t], LANES - HALF + 4 * t, 1) for t in range(3)]
    return list(tiles) + [jnp.where(place < 4, back[0], jnp.where(place < 8, back[1], back[2]))]


def body(
    pair_hbm, d_out_hbm, w_proj_hbm, w_gate_hbm, ow_hbm, out_ref,
    pair_ref, d_out_ref, w_proj_ref, w_gate_ref, ow_ref,
    pad_ref, rows8_ref, rows4_ref, xs_ref, tiles_ref,
    send_a, recv_a, send_b, recv_l, recv_r, send_c, recv_c, send_d, recv_d,
    send_e, recv_e, send_f, send_fz, recv_f, recv_fz, send_g, recv_g, send_h, recv_h,
    in_sem, send_sem, recv_sem, near_sem, far_sem, near_recv, far_recv,
):
    r = lax.axis_index("row")
    c = lax.axis_index("col")
    z_me = r // BLOCK
    q_me = (r // 2) % OWNERS
    is_owner = r % 2 == 0
    not_owner = jnp.logical_not(is_owner)
    barrier = pltpu.get_barrier_semaphore()

    loads = [
        pltpu.make_async_copy(src, dst, in_sem.at[n])
        for n, (src, dst) in enumerate((
            (pair_hbm, pair_ref), (w_proj_hbm, w_proj_ref), (d_out_hbm, d_out_ref),
            (w_gate_hbm, w_gate_ref), (ow_hbm, ow_ref),
        ))
    ]
    for load in loads:
        load.start()

    def greet_col(d, carry):
        pl.semaphore_signal(barrier, inc=1, device_id=(r, lax.rem(c + d, COLS)), device_id_type=MESH)
        return carry

    lax.fori_loop(1, COLS, greet_col, 0)

    @pl.when(is_owner)
    def _():
        def greet_row(d, carry):
            pl.semaphore_signal(barrier, inc=1, device_id=(lax.rem(r + d, ROWS), c), device_id_type=MESH)
            return carry

        lax.fori_loop(1, ROWS, greet_row, 0)

    @pl.when(not_owner)
    def _():
        def greet_owner(n, carry):
            pl.semaphore_signal(barrier, inc=1, device_id=(2 * n, c), device_id_type=MESH)
            return carry

        lax.fori_loop(0, ROWS // 2, greet_owner, 0)

    def padded_transpose(ref):
        for i in range(TILE_I):
            cells = ref[i].astype(F32)
            pad_ref[32 * i : 32 * i + HALF, :] = cells[:HALF]
            pad_ref[32 * i + 16 : 32 * i + 16 + HALF, :] = cells[HALF:]
        return pad_ref[...].T

    def all_to_all(phase, send, recv):
        def one(dz, dx):
            to = lax.rem(c // 4 + dz, 4) * 4 + lax.rem(c + dx, 4)
            pltpu.make_async_remote_copy(
                src_ref=send.at[to], dst_ref=recv.at[c],
                send_sem=send_sem.at[phase], recv_sem=recv_sem.at[phase],
                device_id=(r, to), device_id_type=MESH,
            ).start()

        def opposite(n, carry):
            one(2, n)
            return carry

        def beside(n, carry):
            one(1 + 2 * (n % 2), n // 2)
            return carry

        def same(n, carry):
            one(0, n)
            return carry

        lax.fori_loop(0, 4, opposite, 0)
        lax.fori_loop(0, 8, beside, 0)
        lax.fori_loop(1, 4, same, 0)
        pltpu.make_async_copy(send.at[c], recv.at[c], recv_sem.at[phase]).start()

    def to_near_owners(phase, src_of, dst):
        for q in range(OWNERS):
            owner = z_me * BLOCK + 2 * q

            @pl.when(r == owner)
            def _():
                pltpu.make_async_copy(src_of(q), dst, near_recv.at[phase]).start()

            @pl.when(r != owner)
            def _():
                pltpu.make_async_remote_copy(
                    src_ref=src_of(q), dst_ref=dst,
                    send_sem=near_sem.at[phase, q], recv_sem=near_recv.at[phase],
                    device_id=(owner, c), device_id_type=MESH,
                ).start()

    def to_far_owners(phase, src_of, dst):
        for dz in (3, 1, 2):
            z = lax.rem(z_me + dz, 4)
            for q in range(OWNERS):
                pltpu.make_async_remote_copy(
                    src_ref=src_of(q, z), dst_ref=dst,
                    send_sem=far_sem.at[phase], recv_sem=far_recv.at[phase],
                    device_id=(z * BLOCK + 2 * q, c), device_id_type=MESH,
                ).start()

    def from_owner(phase, send, recv):
        me = r % BLOCK
        pltpu.make_async_copy(send.at[me], recv.at[q_me], near_sem.at[phase, q_me]).start()

        def one(d, carry):
            to = lax.rem(me + d, BLOCK)
            pltpu.make_async_remote_copy(
                src_ref=send.at[to], dst_ref=recv.at[q_me],
                send_sem=send_sem.at[phase], recv_sem=near_sem.at[phase, q_me],
                device_id=(z_me * BLOCK + to, c), device_id_type=MESH,
            ).start()
            return carry

        lax.fori_loop(1, BLOCK, one, 0)

    def wait_all(ref, sem):
        pltpu.make_async_copy(ref, ref, sem).wait()

    def wait_quads(phase, recv):
        for q in range(OWNERS):
            wait_all(recv.at[q], near_sem.at[phase, q])

    def wait_near_sends(phase, src_of):
        for q in range(OWNERS):
            @pl.when(r != z_me * BLOCK + 2 * q)
            def _():
                wait_all(src_of(q), near_sem.at[phase, q])

    def spread(recv, stage, rows):
        for z in range(4):
            for a in range(3):
                parts = [recv[4 * z + x, :, LANES * a : LANES * (a + 1)].astype(F32) for x in range(4)]
                for b, part in enumerate(swap_blocks(parts)):
                    stage[z, pl.ds(4 * a + b, rows, stride=16), :] = part

    def collect(stage, send, rows):
        for z in range(4):
            for a in range(3):
                parts = [stage[z, pl.ds(4 * a + b, rows, stride=16), :] for b in range(4)]
                for x, part in enumerate(swap_blocks(parts)):
                    send[4 * z + x, :, LANES * a : LANES * (a + 1)] = part.astype(BF16)

    pad_ref[...] = jnp.zeros_like(pad_ref)
    rows8_ref[...] = jnp.zeros_like(rows8_ref)
    rows4_ref[...] = jnp.zeros_like(rows4_ref)
    new = lax.broadcasted_iota(jnp.int32, (256, 256), 0)
    old = lax.broadcasted_iota(jnp.int32, (256, 256), 1)
    left_right = new % 2
    q_of = (new // 2) % 4
    col_of = (new // 8) % 16
    value = new // 128
    order = (old == left_right * 128 + value * 64 + col_of * 4 + q_of).astype(F32).astype(BF16)
    eye = (
        lax.broadcasted_iota(jnp.int32, (128, 128), 0) == lax.broadcasted_iota(jnp.int32, (128, 128), 1)
    ).astype(F32).astype(BF16)

    loads[0].wait()
    values = padded_transpose(pair_ref)
    centre = values - jnp.mean(values, axis=0, keepdims=True)
    inv_std = lax.rsqrt(jnp.mean(centre * centre, axis=0, keepdims=True) + EPS)
    zhat = centre * inv_std
    normed = zhat.astype(BF16)
    loads[1].wait()
    w_rows = dot_t(order, w_proj_ref[...]).astype(BF16)
    projected = dot(w_rows, normed)
    gates = jax.nn.sigmoid(projected[:128])
    vals = projected[128:]
    send_a[...] = (gates * vals).astype(BF16).reshape(COLS, 8, 384)

    pl.semaphore_wait(barrier, COLS - 1 + jnp.where(is_owner, ROWS - 1, ROWS // 2))
    all_to_all(0, send_a, recv_a)

    for load in loads[2:]:
        load.wait()
    w_cols = dot_t(w_proj_ref[...], order).astype(BF16)
    w_gate_t = dot_t(eye, w_gate_ref[...]).astype(BF16)
    ow_t = dot_t(eye, ow_ref[...]).astype(BF16)
    upstream = padded_transpose(d_out_ref)
    gate = jax.nn.sigmoid(dot(w_gate_t, normed))
    d_xhat = dot(ow_ref[...], (upstream * gate).astype(BF16))
    d_xhat_mean = jnp.mean(d_xhat, axis=0, keepdims=True)
    gate_slope = upstream * gate * (1.0 - gate)

    wait_all(recv_a, recv_sem.at[0])
    spread(recv_a, rows8_ref, 8)
    for t, tile in enumerate(close_gaps([rows8_ref[z] for z in range(4)])):
        send_b[:, :, t] = tile.astype(BF16).reshape(OWNERS, 2, 16, LANES)
    to_far_owners(0, lambda q, z: send_b.at[q, 1], recv_r.at[r])
    to_near_owners(0, lambda q: send_b.at[q, 1], recv_r.at[r])
    to_near_owners(1, lambda q: send_b.at[q, 0], recv_l.at[r])
    to_far_owners(1, lambda q, z: send_b.at[q, 0], recv_l.at[r])

    def matrix(ref):
        count = ref.shape[0]
        return jnp.concatenate([ref[:, t].reshape(count * 16, LANES) for t in range(3)], axis=1)

    near = pl.ds(pl.multiple_of(z_me * BLOCK, BLOCK), BLOCK)
    others = pl.ds(0, ROWS - BLOCK)

    @pl.when(is_owner)
    def _():
        wait_all(recv_l.at[near], near_recv.at[1])
        wait_all(recv_r.at[near], near_recv.at[0])
        wait_all(recv_r.at[others], far_recv.at[0])
        x_rows = dot_t(matrix(recv_l.at[near]), matrix(recv_r))
        for t, tile in enumerate(close_gaps([x_rows[:, LANES * z : LANES * (z + 1)] for z in range(4)])):
            send_c[:, t] = tile.astype(BF16).reshape(BLOCK, 16, LANES)
        from_owner(2, send_c, recv_c)

    wait_all(send_a.at[pl.ds(0, COLS - 1)], send_sem.at[0])
    wait_quads(2, recv_c)
    tiles = [recv_c[:, t].reshape(OWNERS * 16, LANES).astype(F32) for t in range(3)]
    for z, tile in enumerate(open_gaps(tiles)):
        rows4_ref[z] = tile
    collect(rows4_ref, send_d, 4)
    all_to_all(3, send_d, recv_d)
    wait_near_sends(0, lambda q: send_b.at[q, 1])
    wait_near_sends(1, lambda q: send_b.at[q, 0])
    wait_all(recv_d, recv_sem.at[3])
    for s in range(COLS):
        xs_ref[4 * s : 4 * s + 4, :] = recv_d[s].astype(F32)

    x = xs_ref[...]
    x_centre = x - jnp.mean(x, axis=0, keepdims=True)
    x_inv = lax.rsqrt(jnp.mean(x_centre * x_centre, axis=0, keepdims=True) + EPS)
    xhat = x_centre * x_inv
    d_x = (d_xhat - d_xhat_mean - xhat * jnp.mean(d_xhat * xhat, axis=0, keepdims=True)) * x_inv
    xs_ref[...] = d_x
    for s in range(COLS):
        send_e[s] = xs_ref[4 * s : 4 * s + 4, :].astype(BF16)
    all_to_all(4, send_e, recv_e)

    mixed = dot(ow_t, xhat.astype(BF16))
    d_gate = (mixed * gate_slope).astype(BF16)
    d_normed_gate = dot(w_gate_ref[...], d_gate)
    rows4_ref[...] = jnp.zeros_like(rows4_ref)
    wait_all(send_d.at[pl.ds(0, COLS - 1)], send_sem.at[3])

    wait_all(recv_e, recv_sem.at[4])
    spread(recv_e, rows4_ref, 4)
    for z in range(4):
        send_fz[:, z] = rows4_ref[z].astype(BF16).reshape(OWNERS, 16, LANES)
    for t, tile in enumerate(close_gaps([rows4_ref[z] for z in range(4)])):
        send_f[:, t] = tile.astype(BF16).reshape(OWNERS, 16, LANES)
    to_far_owners(5, lambda q, z: send_fz.at[q, z], recv_fz.at[r])
    to_near_owners(5, lambda q: send_f.at[q], recv_f.at[r % BLOCK])

    @pl.when(is_owner)
    def _():
        wait_all(recv_f, near_recv.at[5])
        tiles = [recv_f[:, t].reshape(BLOCK * 16, LANES).astype(F32) for t in range(3)]
        wide = open_gaps(tiles)
        for z, tile in enumerate(wide):
            tiles_ref[z] = tile
        d_left = dot(jnp.concatenate(wide, axis=1).astype(BF16), matrix(recv_r))
        recv_fz[near] = tiles_ref[z_me].astype(BF16).reshape(BLOCK, 16, LANES)
        for t in range(3):
            send_g[:, 0, t] = d_left[:, LANES * t : LANES * (t + 1)].astype(BF16).reshape(BLOCK, 16, LANES)
        wait_all(recv_l.at[others], far_recv.at[1])
        wait_all(recv_fz.at[others], far_recv.at[5])
        d_x_t = recv_fz[...].reshape(ROWS * 16, LANES).astype(F32).T.astype(BF16)
        d_right = dot(d_x_t, matrix(recv_l))
        for t in range(3):
            send_g[:, 1, t] = d_right[:, LANES * t : LANES * (t + 1)].astype(BF16).reshape(BLOCK, 16, LANES)
        from_owner(6, send_g, recv_g)

    wait_all(send_e.at[pl.ds(0, COLS - 1)], send_sem.at[4])
    wait_all(recv_r.at[pl.ds(0, 12)], far_sem.at[0])
    wait_all(recv_l.at[pl.ds(0, 12)], far_sem.at[1])
    wait_quads(6, recv_g)
    tiles = [recv_g[:, :, t].reshape(OWNERS * 32, LANES).astype(F32) for t in range(3)]
    for z, tile in enumerate(open_gaps(tiles)):
        rows8_ref[z] = tile
    collect(rows8_ref, send_h, 8)
    all_to_all(7, send_h, recv_h)

    wait_near_sends(5, lambda q: send_f.at[q])
    wait_all(recv_fz.at[pl.ds(0, 12)], far_sem.at[5])

    @pl.when(is_owner)
    def _():
        for phase, send in ((2, send_c), (6, send_g)):
            wait_all(send.at[pl.ds(0, BLOCK - 1)], send_sem.at[phase])

    wait_all(recv_h, recv_sem.at[7])

    d_lr = recv_h[...].astype(F32).reshape(COLS * 8, 384)
    d_vals = d_lr * gates
    d_gates = d_vals * vals * (1.0 - gates)
    d_projected = jnp.concatenate([d_gates.astype(BF16), d_vals.astype(BF16)], axis=0)
    d_normed = dot(w_cols, d_projected) + d_normed_gate
    grad_mean = jnp.mean(d_normed, axis=0, keepdims=True)
    cross_mean = jnp.mean(d_normed * zhat, axis=0, keepdims=True)
    pad_ref[...] = ((d_normed - grad_mean - zhat * cross_mean) * inv_std).T
    for i in range(TILE_I):
        out_ref[i, :HALF, :] = pad_ref[32 * i : 32 * i + HALF, :]
        out_ref[i, HALF:, :] = pad_ref[32 * i + 16 : 32 * i + 16 + HALF, :]
    wait_all(send_h.at[pl.ds(0, COLS - 1)], send_sem.at[7])


def per_device(pair, d_out, w_proj, w_gate, output_weight):
    stage1_wide = pltpu.VMEM((COLS, 8, 384), BF16)
    stage1_slim = pltpu.VMEM((COLS, 4, 384), BF16)
    args = (pair, d_out, w_proj, w_gate, output_weight)
    return pl.pallas_call(
        body,
        out_shape=jax.ShapeDtypeStruct(pair.shape, F32),
        in_specs=[pl.BlockSpec(memory_space=pl.ANY)] * 5,
        out_specs=pl.BlockSpec(memory_space=pltpu.VMEM),
        scratch_shapes=[
            *(pltpu.VMEM(a.shape, a.dtype) for a in args),
            pltpu.VMEM((384, LANES), F32),
            pltpu.VMEM((4, 128, LANES), F32),
            pltpu.VMEM((4, 64, LANES), F32),
            pltpu.VMEM((64, 384), F32),
            pltpu.VMEM((4, 128, LANES), F32),
            stage1_wide,
            stage1_wide,
            pltpu.VMEM((OWNERS, 2, 3, 16, LANES), BF16),
            pltpu.VMEM((ROWS, 3, 16, LANES), BF16),
            pltpu.VMEM((ROWS, 3, 16, LANES), BF16),
            pltpu.VMEM((BLOCK, 3, 16, LANES), BF16),
            pltpu.VMEM((OWNERS, 3, 16, LANES), BF16),
            stage1_slim,
            stage1_slim,
            stage1_slim,
            stage1_slim,
            pltpu.VMEM((OWNERS, 3, 16, LANES), BF16),
            pltpu.VMEM((OWNERS, 4, 16, LANES), BF16),
            pltpu.VMEM((BLOCK, 3, 16, LANES), BF16),
            pltpu.VMEM((ROWS, 16, LANES), BF16),
            pltpu.VMEM((BLOCK, 2, 3, 16, LANES), BF16),
            pltpu.VMEM((OWNERS, 2, 3, 16, LANES), BF16),
            stage1_wide,
            stage1_wide,
            pltpu.SemaphoreType.DMA((5,)),
            pltpu.SemaphoreType.DMA((8,)),
            pltpu.SemaphoreType.DMA((8,)),
            pltpu.SemaphoreType.DMA((8, OWNERS)),
            pltpu.SemaphoreType.DMA((8,)),
            pltpu.SemaphoreType.DMA((8,)),
            pltpu.SemaphoreType.DMA((8,)),
        ],
        compiler_params=pltpu.CompilerParams(
            collective_id=0, has_side_effects=True, vmem_limit_bytes=48 * 1024 * 1024
        ),
    )(*args)


def solution(mesh):
    return jax.shard_map(
        per_device,
        mesh=mesh,
        in_specs=(P("row", "col", None), P("row", "col", None), P(), P(), P()),
        out_specs=P("row", "col", None),
        check_vma=False,
    )
```

```python
import functools

import jax
import jax.numpy as jnp
from jax import lax
from jax.experimental import pallas as pl
from jax.experimental.pallas import tpu as pltpu
from jax.sharding import PartitionSpec as P

EPS = 1e-05
MESH = pl.DeviceIdType.MESH
F32 = jnp.float32
BF16 = jnp.bfloat16

ROWS = 32
COLS = 16
OWNERS = 4
BLOCK = 8
HALF = 12
TILE_I = 12
LANES = 128


def dot(a, b):
    return lax.dot_general(a, b, (((1,), (0,)), ((), ())), preferred_element_type=F32)


def dot_t(a, b):
    return lax.dot_general(a, b, (((1,), (1,)), ((), ())), preferred_element_type=F32)


def swap_blocks(parts):
    lane = lax.broadcasted_iota(jnp.int32, parts[0].shape, 1)
    low = lane < 64
    even = (lane // 32) % 2 == 0
    p0, p1, p2, p3 = parts
    t0 = jnp.where(low, p0, pltpu.roll(p2, 64, 1))
    t2 = jnp.where(low, pltpu.roll(p0, 64, 1), p2)
    t1 = jnp.where(low, p1, pltpu.roll(p3, 64, 1))
    t3 = jnp.where(low, pltpu.roll(p1, 64, 1), p3)
    u0 = jnp.where(even, t0, pltpu.roll(t1, 32, 1))
    u1 = jnp.where(even, pltpu.roll(t0, 96, 1), t1)
    u2 = jnp.where(even, t2, pltpu.roll(t3, 32, 1))
    u3 = jnp.where(even, pltpu.roll(t2, 96, 1), t3)
    return u0, u1, u2, u3


def close_gaps(tiles):
    place = lax.broadcasted_iota(jnp.int32, tiles[0].shape, 1) % 16
    return [
        jnp.where(place < HALF, tiles[t], pltpu.roll(tiles[3], HALF - 4 * t, 1)) for t in range(3)
    ]


def open_gaps(tiles):
    place = lax.broadcasted_iota(jnp.int32, tiles[0].shape, 1) % 16
    back = [pltpu.roll(tiles[t], LANES - HALF + 4 * t, 1) for t in range(3)]
    return list(tiles) + [jnp.where(place < 4, back[0], jnp.where(place < 8, back[1], back[2]))]


def body(
    pair_hbm, d_out_hbm, w_proj_hbm, w_gate_hbm, ow_hbm, out_ref,
    pair_ref, d_out_ref, w_proj_ref, w_gate_ref, ow_ref,
    pad_ref, rows8_ref, rows4_ref, xs_ref, tiles_ref,
    send_a, recv_a, send_b, recv_l, recv_r, send_c, recv_c, send_d, recv_d,
    send_e, recv_e, send_f, send_fz, recv_f, recv_fz, send_g, recv_g, send_h, recv_h,
    in_sem, send_sem, recv_sem, near_sem, far_sem, near_recv, far_recv,
):
    r = lax.axis_index("row")
    c = lax.axis_index("col")
    z_me = r // BLOCK
    q_me = (r // 2) % OWNERS
    is_owner = r % 2 == 0
    not_owner = jnp.logical_not(is_owner)
    barrier = pltpu.get_barrier_semaphore()

    loads = [
        pltpu.make_async_copy(src, dst, in_sem.at[n])
        for n, (src, dst) in enumerate((
            (pair_hbm, pair_ref), (w_proj_hbm, w_proj_ref), (d_out_hbm, d_out_ref),
            (w_gate_hbm, w_gate_ref), (ow_hbm, ow_ref),
        ))
    ]
    for load in loads:
        load.start()

    def greet_col(d, carry):
        pl.semaphore_signal(barrier, inc=1, device_id=(r, lax.rem(c + d, COLS)), device_id_type=MESH)
        return carry

    lax.fori_loop(1, COLS, greet_col, 0)

    @pl.when(is_owner)
    def _():
        def greet_row(d, carry):
            pl.semaphore_signal(barrier, inc=1, device_id=(lax.rem(r + d, ROWS), c), device_id_type=MESH)
            return carry

        lax.fori_loop(1, ROWS, greet_row, 0)

    @pl.when(not_owner)
    def _():
        def greet_owner(n, carry):
            pl.semaphore_signal(barrier, inc=1, device_id=(2 * n, c), device_id_type=MESH)
            return carry

        lax.fori_loop(0, ROWS // 2, greet_owner, 0)

    def padded_transpose(ref):
        for i in range(TILE_I):
            cells = ref[i].astype(F32)
            pad_ref[32 * i : 32 * i + HALF, :] = cells[:HALF]
            pad_ref[32 * i + 16 : 32 * i + 16 + HALF, :] = cells[HALF:]
        return pad_ref[...].T

    def all_to_all(phase, send, recv):
        def one(dz, dx):
            to = lax.rem(c // 4 + dz, 4) * 4 + lax.rem(c + dx, 4)
            pltpu.make_async_remote_copy(
                src_ref=send.at[to], dst_ref=recv.at[c],
                send_sem=send_sem.at[phase], recv_sem=recv_sem.at[phase],
                device_id=(r, to), device_id_type=MESH,
            ).start()

        def opposite(n, carry):
            one(2, n)
            return carry

        def beside(n, carry):
            one(1 + 2 * (n % 2), n // 2)
            return carry

        def same(n, carry):
            one(0, n)
            return carry

        lax.fori_loop(0, 4, opposite, 0)
        lax.fori_loop(0, 8, beside, 0)
        lax.fori_loop(1, 4, same, 0)
        pltpu.make_async_copy(send.at[c], recv.at[c], recv_sem.at[phase]).start()

    def to_near_owners(phase, src_of, dst):
        for q in range(OWNERS):
            owner = z_me * BLOCK + 2 * q

            @pl.when(r == owner)
            def _():
                pltpu.make_async_copy(src_of(q), dst, near_recv.at[phase]).start()

            @pl.when(r != owner)
            def _():
                pltpu.make_async_remote_copy(
                    src_ref=src_of(q), dst_ref=dst,
                    send_sem=near_sem.at[phase, q], recv_sem=near_recv.at[phase],
                    device_id=(owner, c), device_id_type=MESH,
                ).start()

    def to_far_owners(phase, src_of, dst):
        for dz in (3, 1, 2):
            z = lax.rem(z_me + dz, 4)
            for q in range(OWNERS):
                pltpu.make_async_remote_copy(
                    src_ref=src_of(q, z), dst_ref=dst,
                    send_sem=far_sem.at[phase], recv_sem=far_recv.at[phase],
                    device_id=(z * BLOCK + 2 * q, c), device_id_type=MESH,
                ).start()

    def from_owner(phase, send, recv):
        me = r % BLOCK
        pltpu.make_async_copy(send.at[me], recv.at[q_me], near_sem.at[phase, q_me]).start()

        def one(d, carry):
            to = lax.rem(me + d, BLOCK)
            pltpu.make_async_remote_copy(
                src_ref=send.at[to], dst_ref=recv.at[q_me],
                send_sem=send_sem.at[phase], recv_sem=near_sem.at[phase, q_me],
                device_id=(z_me * BLOCK + to, c), device_id_type=MESH,
            ).start()
            return carry

        lax.fori_loop(1, BLOCK, one, 0)

    def wait_all(ref, sem):
        pltpu.make_async_copy(ref, ref, sem).wait()

    def wait_quads(phase, recv):
        for q in range(OWNERS):
            wait_all(recv.at[q], near_sem.at[phase, q])

    def wait_near_sends(phase, src_of):
        for q in range(OWNERS):
            @pl.when(r != z_me * BLOCK + 2 * q)
            def _():
                wait_all(src_of(q), near_sem.at[phase, q])

    def spread(recv, stage, rows):
        for z in range(4):
            for a in range(3):
                parts = [recv[4 * z + x, :, LANES * a : LANES * (a + 1)].astype(F32) for x in range(4)]
                for b, part in enumerate(swap_blocks(parts)):
                    stage[z, pl.ds(4 * a + b, rows, stride=16), :] = part

    def collect(stage, send, rows):
        for z in range(4):
            for a in range(3):
                parts = [stage[z, pl.ds(4 * a + b, rows, stride=16), :] for b in range(4)]
                for x, part in enumerate(swap_blocks(parts)):
                    send[4 * z + x, :, LANES * a : LANES * (a + 1)] = part.astype(BF16)

    pad_ref[...] = jnp.zeros_like(pad_ref)
    rows8_ref[...] = jnp.zeros_like(rows8_ref)
    rows4_ref[...] = jnp.zeros_like(rows4_ref)
    new = lax.broadcasted_iota(jnp.int32, (256, 256), 0)
    old = lax.broadcasted_iota(jnp.int32, (256, 256), 1)
    left_right = new % 2
    q_of = (new // 2) % 4
    col_of = (new // 8) % 16
    value = new // 128
    order = (old == left_right * 128 + value * 64 + col_of * 4 + q_of).astype(F32).astype(BF16)
    eye = (
        lax.broadcasted_iota(jnp.int32, (128, 128), 0) == lax.broadcasted_iota(jnp.int32, (128, 128), 1)
    ).astype(F32).astype(BF16)

    loads[0].wait()
    values = padded_transpose(pair_ref)
    centre = values - jnp.mean(values, axis=0, keepdims=True)
    inv_std = lax.rsqrt(jnp.mean(centre * centre, axis=0, keepdims=True) + EPS)
    zhat = centre * inv_std
    normed = zhat.astype(BF16)
    loads[1].wait()
    w_rows = dot_t(order, w_proj_ref[...]).astype(BF16)
    projected = dot(w_rows, normed)
    gates = jax.nn.sigmoid(projected[:128])
    vals = projected[128:]
    send_a[...] = (gates * vals).astype(BF16).reshape(COLS, 8, 384)

    pl.semaphore_wait(barrier, COLS - 1 + jnp.where(is_owner, ROWS - 1, ROWS // 2))
    all_to_all(0, send_a, recv_a)

    for load in loads[2:]:
        load.wait()
    w_cols = dot_t(w_proj_ref[...], order).astype(BF16)
    w_gate_t = dot_t(eye, w_gate_ref[...]).astype(BF16)
    ow_t = dot_t(eye, ow_ref[...]).astype(BF16)
    upstream = padded_transpose(d_out_ref)
    gate = jax.nn.sigmoid(dot(w_gate_t, normed))
    d_xhat = dot(ow_ref[...], (upstream * gate).astype(BF16))
    d_xhat_mean = jnp.mean(d_xhat, axis=0, keepdims=True)
    gate_slope = upstream * gate * (1.0 - gate)

    wait_all(recv_a, recv_sem.at[0])
    spread(recv_a, rows8_ref, 8)
    for t, tile in enumerate(close_gaps([rows8_ref[z] for z in range(4)])):
        send_b[:, :, t] = tile.astype(BF16).reshape(OWNERS, 2, 16, LANES)
    to_far_owners(0, lambda q, z: send_b.at[q, 1], recv_r.at[r])
    to_near_owners(0, lambda q: send_b.at[q, 1], recv_r.at[r])
    to_near_owners(1, lambda q: send_b.at[q, 0], recv_l.at[r])
    to_far_owners(1, lambda q, z: send_b.at[q, 0], recv_l.at[r])

    def matrix(ref):
        count = ref.shape[0]
        return jnp.concatenate([ref[:, t].reshape(count * 16, LANES) for t in range(3)], axis=1)

    near = pl.ds(pl.multiple_of(z_me * BLOCK, BLOCK), BLOCK)
    others = pl.ds(0, ROWS - BLOCK)

    @pl.when(is_owner)
    def _():
        wait_all(recv_l.at[near], near_recv.at[1])
        wait_all(recv_r.at[near], near_recv.at[0])
        wait_all(recv_r.at[others], far_recv.at[0])
        x_rows = dot_t(matrix(recv_l.at[near]), matrix(recv_r))
        for t, tile in enumerate(close_gaps([x_rows[:, LANES * z : LANES * (z + 1)] for z in range(4)])):
            send_c[:, t] = tile.astype(BF16).reshape(BLOCK, 16, LANES)
        from_owner(2, send_c, recv_c)

    wait_all(send_a.at[pl.ds(0, COLS - 1)], send_sem.at[0])
    wait_quads(2, recv_c)
    tiles = [recv_c[:, t].reshape(OWNERS * 16, LANES).astype(F32) for t in range(3)]
    for z, tile in enumerate(open_gaps(tiles)):
        rows4_ref[z] = tile
    collect(rows4_ref, send_d, 4)
    all_to_all(3, send_d, recv_d)
    wait_near_sends(0, lambda q: send_b.at[q, 1])
    wait_near_sends(1, lambda q: send_b.at[q, 0])
    wait_all(recv_d, recv_sem.at[3])
    for s in range(COLS):
        xs_ref[4 * s : 4 * s + 4, :] = recv_d[s].astype(F32)

    x = xs_ref[...]
    x_centre = x - jnp.mean(x, axis=0, keepdims=True)
    x_inv = lax.rsqrt(jnp.mean(x_centre * x_centre, axis=0, keepdims=True) + EPS)
    xhat = x_centre * x_inv
    d_x = (d_xhat - d_xhat_mean - xhat * jnp.mean(d_xhat * xhat, axis=0, keepdims=True)) * x_inv
    xs_ref[...] = d_x
    for s in range(COLS):
        send_e[s] = xs_ref[4 * s : 4 * s + 4, :].astype(BF16)
    all_to_all(4, send_e, recv_e)

    mixed = dot(ow_t, xhat.astype(BF16))
    d_gate = (mixed * gate_slope).astype(BF16)
    d_normed_gate = dot(w_gate_ref[...], d_gate)
    rows4_ref[...] = jnp.zeros_like(rows4_ref)
    wait_all(send_d.at[pl.ds(0, COLS - 1)], send_sem.at[3])

    wait_all(recv_e, recv_sem.at[4])
    spread(recv_e, rows4_ref, 4)
    for z in range(4):
        send_fz[:, z] = rows4_ref[z].astype(BF16).reshape(OWNERS, 16, LANES)
    for t, tile in enumerate(close_gaps([rows4_ref[z] for z in range(4)])):
        send_f[:, t] = tile.astype(BF16).reshape(OWNERS, 16, LANES)
    to_far_owners(5, lambda q, z: send_fz.at[q, z], recv_fz.at[r])
    to_near_owners(5, lambda q: send_f.at[q], recv_f.at[r % BLOCK])

    @pl.when(is_owner)
    def _():
        wait_all(recv_f, near_recv.at[5])
        tiles = [recv_f[:, t].reshape(BLOCK * 16, LANES).astype(F32) for t in range(3)]
        wide = open_gaps(tiles)
        for z, tile in enumerate(wide):
            tiles_ref[z] = tile
        d_left = dot(jnp.concatenate(wide, axis=1).astype(BF16), matrix(recv_r))
        recv_fz[near] = tiles_ref[z_me].astype(BF16).reshape(BLOCK, 16, LANES)
        for t in range(3):
            send_g[:, 0, t] = d_left[:, LANES * t : LANES * (t + 1)].astype(BF16).reshape(BLOCK, 16, LANES)
        wait_all(recv_l.at[others], far_recv.at[1])
        wait_all(recv_fz.at[others], far_recv.at[5])
        d_x_t = recv_fz[...].reshape(ROWS * 16, LANES).astype(F32).T.astype(BF16)
        d_right = dot(d_x_t, matrix(recv_l))
        for t in range(3):
            send_g[:, 1, t] = d_right[:, LANES * t : LANES * (t + 1)].astype(BF16).reshape(BLOCK, 16, LANES)
        from_owner(6, send_g, recv_g)

    wait_all(send_e.at[pl.ds(0, COLS - 1)], send_sem.at[4])
    wait_all(recv_r.at[pl.ds(0, 12)], far_sem.at[0])
    wait_all(recv_l.at[pl.ds(0, 12)], far_sem.at[1])
    wait_quads(6, recv_g)
    tiles = [recv_g[:, :, t].reshape(OWNERS * 32, LANES).astype(F32) for t in range(3)]
    for z, tile in enumerate(open_gaps(tiles)):
        rows8_ref[z] = tile
    collect(rows8_ref, send_h, 8)
    all_to_all(7, send_h, recv_h)

    wait_near_sends(5, lambda q: send_f.at[q])
    wait_all(recv_fz.at[pl.ds(0, 12)], far_sem.at[5])

    @pl.when(is_owner)
    def _():
        for phase, send in ((2, send_c), (6, send_g)):
            wait_all(send.at[pl.ds(0, BLOCK - 1)], send_sem.at[phase])

    wait_all(recv_h, recv_sem.at[7])

    d_lr = recv_h[...].astype(F32).reshape(COLS * 8, 384)
    d_vals = d_lr * gates
    d_gates = d_vals * vals * (1.0 - gates)
    d_projected = jnp.concatenate([d_gates.astype(BF16), d_vals.astype(BF16)], axis=0)
    d_normed = dot(w_cols, d_projected) + d_normed_gate
    grad_mean = jnp.mean(d_normed, axis=0, keepdims=True)
    cross_mean = jnp.mean(d_normed * zhat, axis=0, keepdims=True)
    pad_ref[...] = ((d_normed - grad_mean - zhat * cross_mean) * inv_std).T
    for i in range(TILE_I):
        out_ref[i, :HALF, :] = pad_ref[32 * i : 32 * i + HALF, :]
        out_ref[i, HALF:, :] = pad_ref[32 * i + 16 : 32 * i + 16 + HALF, :]
    wait_all(send_h.at[pl.ds(0, COLS - 1)], send_sem.at[7])


def per_device(pair, d_out, w_proj, w_gate, output_weight):
    stage1_wide = pltpu.VMEM((COLS, 8, 384), BF16)
    stage1_slim = pltpu.VMEM((COLS, 4, 384), BF16)
    args = (pair, d_out, w_proj, w_gate, output_weight)
    return pl.pallas_call(
        body,
        out_shape=jax.ShapeDtypeStruct(pair.shape, F32),
        in_specs=[pl.BlockSpec(memory_space=pltpu.HBM)] * 5,
        out_specs=pl.BlockSpec(memory_space=pltpu.VMEM),
        scratch_shapes=[
            *(pltpu.VMEM(a.shape, a.dtype) for a in args),
            pltpu.VMEM((384, LANES), F32),
            pltpu.VMEM((4, 128, LANES), F32),
            pltpu.VMEM((4, 64, LANES), F32),
            pltpu.VMEM((64, 384), F32),
            pltpu.VMEM((4, 128, LANES), F32),
            stage1_wide,
            stage1_wide,
            pltpu.VMEM((OWNERS, 2, 3, 16, LANES), BF16),
            pltpu.VMEM((ROWS, 3, 16, LANES), BF16),
            pltpu.VMEM((ROWS, 3, 16, LANES), BF16),
            pltpu.VMEM((BLOCK, 3, 16, LANES), BF16),
            pltpu.VMEM((OWNERS, 3, 16, LANES), BF16),
            stage1_slim,
            stage1_slim,
            stage1_slim,
            stage1_slim,
            pltpu.VMEM((OWNERS, 3, 16, LANES), BF16),
            pltpu.VMEM((OWNERS, 4, 16, LANES), BF16),
            pltpu.VMEM((BLOCK, 3, 16, LANES), BF16),
            pltpu.VMEM((ROWS, 16, LANES), BF16),
            pltpu.VMEM((BLOCK, 2, 3, 16, LANES), BF16),
            pltpu.VMEM((OWNERS, 2, 3, 16, LANES), BF16),
            stage1_wide,
            stage1_wide,
            pltpu.SemaphoreType.DMA((5,)),
            pltpu.SemaphoreType.DMA((8,)),
            pltpu.SemaphoreType.DMA((8,)),
            pltpu.SemaphoreType.DMA((8, OWNERS)),
            pltpu.SemaphoreType.DMA((8,)),
            pltpu.SemaphoreType.DMA((8,)),
            pltpu.SemaphoreType.DMA((8,)),
        ],
        compiler_params=pltpu.CompilerParams(
            collective_id=0, has_side_effects=True, vmem_limit_bytes=60 * 1024 * 1024
        ),
    )(*args)


def solution(mesh):
    return jax.shard_map(
        per_device,
        mesh=mesh,
        in_specs=(P("row", "col", None), P("row", "col", None), P(), P(), P()),
        out_specs=P("row", "col", None),
        check_vma=False,
    )
```

```python
import jax
import jax.numpy as jnp
from jax import lax
from jax.experimental import pallas as pl
from jax.experimental.pallas import tpu as pltpu
from jax.sharding import PartitionSpec as P

EPS = 1e-05
MESH = pl.DeviceIdType.MESH
F32 = jnp.float32
BF16 = jnp.bfloat16

LANES = 128
GROUP = 64
PEERS = 8
HALF = 12
TILE_I = 12
CELLS = 384
TILES = CELLS // LANES


def dot(a, b):
    return lax.dot_general(a, b, (((1,), (0,)), ((), ())), preferred_element_type=F32)


def dot_t(a, b):
    return lax.dot_general(a, b, (((1,), (1,)), ((), ())), preferred_element_type=F32)


def swap_blocks(parts):
    lane = lax.broadcasted_iota(jnp.int32, parts[0].shape, 1)
    low = lane < 64
    even = (lane // 32) % 2 == 0
    p0, p1, p2, p3 = parts
    t0 = jnp.where(low, p0, pltpu.roll(p2, 64, 1))
    t2 = jnp.where(low, pltpu.roll(p0, 64, 1), p2)
    t1 = jnp.where(low, p1, pltpu.roll(p3, 64, 1))
    t3 = jnp.where(low, pltpu.roll(p1, 64, 1), p3)
    u0 = jnp.where(even, t0, pltpu.roll(t1, 32, 1))
    u1 = jnp.where(even, pltpu.roll(t0, 96, 1), t1)
    u2 = jnp.where(even, t2, pltpu.roll(t3, 32, 1))
    u3 = jnp.where(even, pltpu.roll(t2, 96, 1), t3)
    return u0, u1, u2, u3


def close_gaps(tiles):
    place = lax.broadcasted_iota(jnp.int32, tiles[0].shape, 1) % 16
    return [
        jnp.where(place < HALF, tiles[t], pltpu.roll(tiles[3], HALF - 4 * t, 1)) for t in range(3)
    ]


def open_gaps(tiles):
    place = lax.broadcasted_iota(jnp.int32, tiles[0].shape, 1) % 16
    back = [pltpu.roll(tiles[t], LANES - HALF + 4 * t, 1) for t in range(3)]
    return list(tiles) + [jnp.where(place < 4, back[0], jnp.where(place < 8, back[1], back[2]))]


def body(
    pair_hbm, d_out_hbm, w_proj_hbm, w_gate_hbm, ow_hbm, out_ref,
    pair_ref, d_out_ref, w_proj_ref, w_gate_ref, ow_ref,
    pad_ref, slots8_ref, slots4_ref, rows8_ref, rows4_ref,
    send_a, recv_a, recv_l, recv_r, send_d, recv_d, send_e, recv_e, send_f, recv_f, send_h, recv_h,
    in_sem, send_sem, recv_sem,
):
    r = lax.axis_index("row")
    c = lax.axis_index("col")
    peer = lax.rem(r, PEERS)
    x_me = lax.rem(c, 4)
    z_lo = r // PEERS
    z_me = (c // 4) * 4 + z_lo
    slot = (c // 4) * 16 + x_me * 4 + z_lo
    barrier = pltpu.get_barrier_semaphore()

    loads = [
        pltpu.make_async_copy(src, dst, in_sem.at[n])
        for n, (src, dst) in enumerate((
            (pair_hbm, pair_ref), (w_proj_hbm, w_proj_ref), (d_out_hbm, d_out_ref),
            (w_gate_hbm, w_gate_ref), (ow_hbm, ow_ref),
        ))
    ]
    for load in loads:
        load.start()

    def each_of_group(act):
        def at(dz, dx):
            z = lax.rem(z_me + dz, 16)
            x = lax.rem(x_me + dx, 4)
            act((lax.rem(z, 4) * PEERS + peer, (z // 4) * 4 + x), (z // 4) * 16 + x * 4 + lax.rem(z, 4))

        def step(n, carry):
            away = (n + 1) // 2
            dz = 8 + jnp.where(lax.rem(n, 2) == 1, away, -away)
            for dx in (2, 1, 3, 0):
                at(dz, dx)
            return carry

        lax.fori_loop(0, 15, step, 0)
        for dx in (2, 1, 3):
            at(0, dx)

    def each_peer(act):
        def step(d, carry):
            to = lax.rem(peer + d, PEERS)
            act((z_lo * PEERS + to, c), to)
            return carry

        lax.fori_loop(1, PEERS, step, 0)

    def greet(device, _):
        pl.semaphore_signal(barrier, inc=1, device_id=device, device_id_type=MESH)

    each_of_group(greet)
    each_peer(greet)

    def wait_all(ref, sem):
        pltpu.make_async_copy(ref, ref, sem).wait()

    def exchange(phase, send, recv):
        def one(device, to):
            pltpu.make_async_remote_copy(
                src_ref=send.at[to], dst_ref=recv.at[slot],
                send_sem=send_sem.at[phase], recv_sem=recv_sem.at[phase],
                device_id=device, device_id_type=MESH,
            ).start()

        each_of_group(one)
        pltpu.make_async_copy(send.at[slot], recv.at[slot], recv_sem.at[phase]).start()

    def share(phase, src_of, recv):
        def one(device, to):
            pltpu.make_async_remote_copy(
                src_ref=src_of(to), dst_ref=recv.at[peer],
                send_sem=send_sem.at[phase], recv_sem=recv_sem.at[phase],
                device_id=device, device_id_type=MESH,
            ).start()

        each_peer(one)

    def wait_sends(phase, ref):
        wait_all(ref.at[pl.ds(0, ref.shape[0] - 1)], send_sem.at[phase])

    def padded_transpose(ref):
        for i in range(TILE_I):
            cells = ref[i].astype(F32)
            pad_ref[32 * i : 32 * i + HALF, :] = cells[:HALF]
            pad_ref[32 * i + 16 : 32 * i + 16 + HALF, :] = cells[HALF:]
        return pad_ref[...].T

    def tile_of(array, t):
        return array[:, LANES * t : LANES * (t + 1)]

    pad_ref[...] = jnp.zeros_like(pad_ref)
    slots8_ref[...] = jnp.zeros_like(slots8_ref)
    slots4_ref[...] = jnp.zeros_like(slots4_ref)
    new = lax.broadcasted_iota(jnp.int32, (256, 256), 0)
    old = lax.broadcasted_iota(jnp.int32, (256, 256), 1)
    order = (old == (new % 2) * 128 + (new // 128) * 64 + (new // 2) % 64).astype(F32).astype(BF16)
    eye = (
        lax.broadcasted_iota(jnp.int32, (128, 128), 0) == lax.broadcasted_iota(jnp.int32, (128, 128), 1)
    ).astype(F32).astype(BF16)

    loads[0].wait()
    values = padded_transpose(pair_ref)
    centre = values - jnp.mean(values, axis=0, keepdims=True)
    inv_std = lax.rsqrt(jnp.mean(centre * centre, axis=0, keepdims=True) + EPS)
    zhat = centre * inv_std
    normed = zhat.astype(BF16)
    loads[1].wait()
    w_rows = dot_t(order, w_proj_ref[...]).astype(BF16)
    projected = dot(w_rows, normed)
    gates = jax.nn.sigmoid(projected[:128])
    vals = projected[128:]
    left_right = gates * vals
    for a in range(TILES):
        slots8_ref[pl.ds(a, 128, stride=4), :] = tile_of(left_right, a)
    send_a[...] = slots8_ref[...].astype(BF16).reshape(GROUP, 8, LANES)

    pl.semaphore_wait(barrier, GROUP - 1 + PEERS - 1)
    exchange(0, send_a, recv_a)

    for load in loads[2:]:
        load.wait()
    w_cols = dot_t(w_proj_ref[...], order).astype(BF16)
    w_gate_t = dot_t(eye, w_gate_ref[...]).astype(BF16)
    ow_t = dot_t(eye, ow_ref[...]).astype(BF16)
    upstream = padded_transpose(d_out_ref)
    gate = jax.nn.sigmoid(dot(w_gate_t, normed))
    d_xhat = dot(ow_ref[...], (upstream * gate).astype(BF16))
    d_xhat_mean = jnp.mean(d_xhat, axis=0, keepdims=True)
    gate_slope = upstream * gate * (1.0 - gate)

    wait_all(recv_a, recv_sem.at[0])
    for zh in range(4):
        for zl in range(4):
            parts = [recv_a[16 * zh + 4 * x + zl].astype(F32) for x in range(4)]
            for b, part in enumerate(swap_blocks(parts)):
                rows8_ref[zh, pl.ds(32 * zl + b, 8, stride=4), :] = part
    for t, tile in enumerate(close_gaps([rows8_ref[zh] for zh in range(4)])):
        both = tile.astype(BF16).reshape(4, 2, 16, LANES)
        recv_l[peer, :, t] = both[:, 0]
        recv_r[peer, :, t] = both[:, 1]
    share(1, lambda to: recv_r.at[peer], recv_r)
    share(2, lambda to: recv_l.at[peer], recv_l)

    def own_rows(ref):
        return jnp.concatenate([ref[peer, :, t].reshape(64, LANES) for t in range(TILES)], axis=1)

    def all_rows(ref):
        return jnp.concatenate(
            [
                jnp.concatenate([ref[:, zl, t].reshape(128, LANES) for zl in range(4)], axis=0)
                for t in range(TILES)
            ],
            axis=1,
        )

    wait_sends(0, send_a)
    wait_all(recv_r.at[pl.ds(0, PEERS - 1)], recv_sem.at[1])
    right = all_rows(recv_r)
    x_rows = dot_t(own_rows(recv_l), right)
    for zh in range(4):
        rows4_ref[zh] = tile_of(x_rows, zh)
    for zh in range(4):
        for pair in range(2):
            parts = [rows4_ref[zh, pl.ds(32 * pair + b, 8, stride=4), :] for b in range(4)]
            for x, part in enumerate(swap_blocks(parts)):
                first = 16 * zh + 4 * x + 2 * pair
                send_d[first] = part[:4].astype(BF16)
                send_d[first + 1] = part[4:].astype(BF16)
    exchange(3, send_d, recv_d)
    wait_sends(1, recv_r)
    wait_all(recv_d, recv_sem.at[3])

    for n in range(GROUP):
        slots4_ref[4 * n : 4 * n + 4, :] = recv_d[n].astype(F32)
    x = jnp.concatenate([slots4_ref[pl.ds(a, GROUP, stride=4), :] for a in range(TILES)], axis=1)
    x_centre = x - jnp.mean(x, axis=0, keepdims=True)
    x_inv = lax.rsqrt(jnp.mean(x_centre * x_centre, axis=0, keepdims=True) + EPS)
    xhat = x_centre * x_inv
    d_x = (d_xhat - d_xhat_mean - xhat * jnp.mean(d_xhat * xhat, axis=0, keepdims=True)) * x_inv
    slots4_ref[...] = jnp.zeros_like(slots4_ref)
    for a in range(TILES):
        slots4_ref[pl.ds(a, GROUP, stride=4), :] = tile_of(d_x, a)
    for n in range(GROUP):
        send_e[n] = slots4_ref[4 * n : 4 * n + 4, :].astype(BF16)
    exchange(4, send_e, recv_e)

    mixed = dot(ow_t, xhat.astype(BF16))
    d_gate = (mixed * gate_slope).astype(BF16)
    d_normed_gate = dot(w_gate_ref[...], d_gate)
    wait_sends(2, recv_l)
    wait_sends(3, send_d)

    wait_all(recv_e, recv_sem.at[4])
    for zh in range(4):
        for pair in range(2):
            parts = []
            for x in range(4):
                first = 16 * zh + 4 * x + 2 * pair
                parts.append(jnp.concatenate([recv_e[first].astype(F32), recv_e[first + 1].astype(F32)], axis=0))
            for b, part in enumerate(swap_blocks(parts)):
                rows4_ref[zh, pl.ds(32 * pair + b, 8, stride=4), :] = part
    d_x_rows = jnp.concatenate([rows4_ref[zh] for zh in range(4)], axis=1)
    d_x_cols = jnp.concatenate([d_x_rows, jnp.zeros_like(d_x_rows)], axis=0).T.astype(BF16)
    d_x_cols = d_x_cols.reshape(4, PEERS, 16, LANES)
    for to in range(PEERS):
        send_f[to] = d_x_cols[:, to]
    recv_f[peer] = send_f[peer]
    share(5, lambda to: send_f.at[to], recv_f)

    d_left = dot(d_x_rows.astype(BF16), right)
    for zh, tile in enumerate(open_gaps([tile_of(d_left, t) for t in range(TILES)])):
        for zl in range(4):
            rows8_ref[zh, 32 * zl : 32 * zl + 16, :] = tile[16 * zl : 16 * zl + 16]
    wait_sends(4, send_e)
    wait_all(recv_l.at[pl.ds(0, PEERS - 1)], recv_sem.at[2])
    wait_all(recv_f.at[pl.ds(0, PEERS - 1)], recv_sem.at[5])
    d_right = None
    for g in range(PEERS):
        left_g = jnp.concatenate([recv_l[g, :, t].reshape(64, LANES) for t in range(TILES)], axis=1)
        term = dot(recv_f[g].reshape(64, LANES)[:, :64], left_g)
        d_right = term if d_right is None else d_right + term
    for zh, tile in enumerate(open_gaps([tile_of(d_right, t) for t in range(TILES)])):
        for zl in range(4):
            rows8_ref[zh, 32 * zl + 16 : 32 * zl + 32, :] = tile[16 * zl : 16 * zl + 16]
    for zh in range(4):
        for zl in range(4):
            parts = [rows8_ref[zh, pl.ds(32 * zl + b, 8, stride=4), :] for b in range(4)]
            for x, part in enumerate(swap_blocks(parts)):
                send_h[16 * zh + 4 * x + zl] = part.astype(BF16)
    exchange(6, send_h, recv_h)
    wait_sends(5, send_f)
    wait_all(recv_h, recv_sem.at[6])

    slots8_ref[...] = recv_h[...].astype(F32).reshape(GROUP * 8, LANES)
    d_lr = jnp.concatenate([slots8_ref[pl.ds(a, 128, stride=4), :] for a in range(TILES)], axis=1)
    d_vals = d_lr * gates
    d_gates = d_vals * vals * (1.0 - gates)
    d_projected = jnp.concatenate([d_gates.astype(BF16), d_vals.astype(BF16)], axis=0)
    d_normed = dot(w_cols, d_projected) + d_normed_gate
    grad_mean = jnp.mean(d_normed, axis=0, keepdims=True)
    cross_mean = jnp.mean(d_normed * zhat, axis=0, keepdims=True)
    pad_ref[...] = ((d_normed - grad_mean - zhat * cross_mean) * inv_std).T
    for i in range(TILE_I):
        out_ref[i, :HALF, :] = pad_ref[32 * i : 32 * i + HALF, :]
        out_ref[i, HALF:, :] = pad_ref[32 * i + 16 : 32 * i + 16 + HALF, :]
    wait_sends(6, send_h)


def per_device(pair, d_out, w_proj, w_gate, output_weight):
    slots8 = pltpu.VMEM((GROUP, 8, LANES), BF16)
    slots4 = pltpu.VMEM((GROUP, 4, LANES), BF16)
    rows = pltpu.VMEM((PEERS, 4, TILES, 16, LANES), BF16)
    blocks = pltpu.VMEM((PEERS, 4, 16, LANES), BF16)
    args = (pair, d_out, w_proj, w_gate, output_weight)
    return pl.pallas_call(
        body,
        out_shape=jax.ShapeDtypeStruct(pair.shape, F32),
        in_specs=[pl.BlockSpec(memory_space=pltpu.HBM)] * 5,
        out_specs=pl.BlockSpec(memory_space=pltpu.VMEM),
        scratch_shapes=[
            *(pltpu.VMEM(a.shape, a.dtype) for a in args),
            pltpu.VMEM((CELLS, LANES), F32),
            pltpu.VMEM((GROUP * 8, LANES), F32),
            pltpu.VMEM((GROUP * 4, LANES), F32),
            pltpu.VMEM((4, 128, LANES), F32),
            pltpu.VMEM((4, 64, LANES), F32),
            slots8, slots8,
            rows, rows,
            slots4, slots4,
            slots4, slots4,
            blocks, blocks,
            slots8, slots8,
            pltpu.SemaphoreType.DMA((5,)),
            pltpu.SemaphoreType.DMA((7,)),
            pltpu.SemaphoreType.DMA((7,)),
        ],
        compiler_params=pltpu.CompilerParams(
            collective_id=0, has_side_effects=True, vmem_limit_bytes=60 * 1024 * 1024
        ),
    )(*args)


def solution(mesh):
    return jax.shard_map(
        per_device,
        mesh=mesh,
        in_specs=(P("row", "col", None), P("row", "col", None), P(), P(), P()),
        out_specs=P("row", "col", None),
        check_vma=False,
    )
```

```python
import jax
import jax.numpy as jnp
from jax import lax
from jax.experimental import pallas as pl
from jax.experimental.pallas import tpu as pltpu
from jax.sharding import PartitionSpec as P

EPS = 1e-05
MESH = pl.DeviceIdType.MESH
F32 = jnp.float32
BF16 = jnp.bfloat16

LANES = 128
GROUP = 64
PEERS = 8
HALF = 12
TILE_I = 12
CELLS = 384
TILES = CELLS // LANES


def dot(a, b):
    return lax.dot_general(a, b, (((1,), (0,)), ((), ())), preferred_element_type=F32)


def dot_t(a, b):
    return lax.dot_general(a, b, (((1,), (1,)), ((), ())), preferred_element_type=F32)


def swap_blocks(parts):
    lane = lax.broadcasted_iota(jnp.int32, parts[0].shape, 1)
    low = lane < 64
    even = (lane // 32) % 2 == 0
    p0, p1, p2, p3 = parts
    t0 = jnp.where(low, p0, pltpu.roll(p2, 64, 1))
    t2 = jnp.where(low, pltpu.roll(p0, 64, 1), p2)
    t1 = jnp.where(low, p1, pltpu.roll(p3, 64, 1))
    t3 = jnp.where(low, pltpu.roll(p1, 64, 1), p3)
    u0 = jnp.where(even, t0, pltpu.roll(t1, 32, 1))
    u1 = jnp.where(even, pltpu.roll(t0, 96, 1), t1)
    u2 = jnp.where(even, t2, pltpu.roll(t3, 32, 1))
    u3 = jnp.where(even, pltpu.roll(t2, 96, 1), t3)
    return u0, u1, u2, u3


def close_gaps(tiles):
    place = lax.broadcasted_iota(jnp.int32, tiles[0].shape, 1) % 16
    return [
        jnp.where(place < HALF, tiles[t], pltpu.roll(tiles[3], HALF - 4 * t, 1)) for t in range(3)
    ]


def open_gaps(tiles):
    place = lax.broadcasted_iota(jnp.int32, tiles[0].shape, 1) % 16
    back = [pltpu.roll(tiles[t], LANES - HALF + 4 * t, 1) for t in range(3)]
    return list(tiles) + [jnp.where(place < 4, back[0], jnp.where(place < 8, back[1], back[2]))]


def body(
    pair_hbm, d_out_hbm, w_proj_hbm, w_gate_hbm, ow_hbm, out_ref,
    pair_ref, d_out_ref, w_proj_ref, w_gate_ref, ow_ref,
    pad_ref, slots_ref, rows_ref, left_ref, right_ref,
    send_a, recv_a, send_b, recv_b, send_d, recv_d, send_e, recv_e, send_f, recv_f, send_g, recv_g, send_h, recv_h,
    in_sem, send_sem, recv_sem,
):
    r = lax.axis_index("row")
    c = lax.axis_index("col")
    peer = lax.rem(r, PEERS)
    x_me = lax.rem(c, 4)
    z_lo = r // PEERS
    z_me = (c // 4) * 4 + z_lo
    slot = (c // 4) * 16 + x_me * 4 + z_lo
    barrier = pltpu.get_barrier_semaphore()

    def each_of_group(act):
        def at(dz, dx):
            z = lax.rem(z_me + dz, 16)
            x = lax.rem(x_me + dx, 4)
            act((lax.rem(z, 4) * PEERS + peer, (z // 4) * 4 + x), (z // 4) * 16 + x * 4 + lax.rem(z, 4))

        def step(n, carry):
            away = (n + 1) // 2
            dz = 8 + jnp.where(lax.rem(n, 2) == 1, away, -away)
            for dx in (2, 1, 3, 0):
                at(dz, dx)
            return carry

        lax.fori_loop(0, 15, step, 0)
        for dx in (2, 1, 3):
            at(0, dx)

    def each_peer(act):
        def step(d, carry):
            to = lax.rem(peer + d, PEERS)
            act((z_lo * PEERS + to, c), to)
            return carry

        lax.fori_loop(1, PEERS, step, 0)

    def greet(device, _):
        pl.semaphore_signal(barrier, inc=1, device_id=device, device_id_type=MESH)

    each_of_group(greet)
    each_peer(greet)

    loads = [
        pltpu.make_async_copy(src, dst, in_sem.at[n])
        for n, (src, dst) in enumerate((
            (pair_hbm, pair_ref), (w_proj_hbm, w_proj_ref), (d_out_hbm, d_out_ref),
            (w_gate_hbm, w_gate_ref), (ow_hbm, ow_ref),
        ))
    ]
    for load in loads:
        load.start()

    def wait_all(ref, sem):
        pltpu.make_async_copy(ref, ref, sem).wait()

    def exchange(phase, send, recv):
        def one(device, to):
            pltpu.make_async_remote_copy(
                src_ref=send.at[to], dst_ref=recv.at[slot],
                send_sem=send_sem.at[phase], recv_sem=recv_sem.at[phase],
                device_id=device, device_id_type=MESH,
            ).start()

        each_of_group(one)
        pltpu.make_async_copy(send.at[slot], recv.at[slot], recv_sem.at[phase]).start()

    def share(phase, src_of, recv):
        def one(device, to):
            pltpu.make_async_remote_copy(
                src_ref=src_of(to), dst_ref=recv.at[peer],
                send_sem=send_sem.at[phase], recv_sem=recv_sem.at[phase],
                device_id=device, device_id_type=MESH,
            ).start()

        each_peer(one)

    def wait_sends(phase, ref):
        wait_all(ref.at[pl.ds(0, ref.shape[0] - 1)], send_sem.at[phase])

    def padded_transpose(ref):
        for i in range(TILE_I):
            cells = ref[i].astype(F32)
            pad_ref[32 * i : 32 * i + HALF, :] = cells[:HALF]
            pad_ref[32 * i + 16 : 32 * i + 16 + HALF, :] = cells[HALF:]
        return pad_ref[...].T

    def tile_of(array, t):
        return array[:, LANES * t : LANES * (t + 1)]

    def to_slots(array, send):
        for a in range(TILES):
            slots_ref[pl.ds(a, GROUP, stride=4), :] = tile_of(array, a)
        for n in range(GROUP):
            send[n] = slots_ref[4 * n : 4 * n + 4, :].astype(BF16)

    def from_slots(recv):
        for n in range(GROUP):
            slots_ref[4 * n : 4 * n + 4, :] = recv[n].astype(F32)
        return jnp.concatenate([slots_ref[pl.ds(a, GROUP, stride=4), :] for a in range(TILES)], axis=1)

    def gather_rows(recv):
        for zh in range(4):
            for pair in range(2):
                parts = []
                for x in range(4):
                    first = 16 * zh + 4 * x + 2 * pair
                    parts.append(jnp.concatenate([recv[first].astype(F32), recv[first + 1].astype(F32)], axis=0))
                for b, part in enumerate(swap_blocks(parts)):
                    rows_ref[zh, pl.ds(32 * pair + b, 8, stride=4), :] = part
            for zl in range(3):
                rows_ref[zh, 16 * zl + HALF : 16 * zl + 16, :] = rows_ref[zh, 48 + 4 * zl : 52 + 4 * zl, :]
        return close_gaps([rows_ref[zh, :48, :] for zh in range(4)])

    def scatter_rows(array, send):
        for zh, tile in enumerate(open_gaps([tile_of(array, t) for t in range(TILES)])):
            rows_ref[zh, :48, :] = tile
            for zl in range(3):
                rows_ref[zh, 48 + 4 * zl : 52 + 4 * zl, :] = rows_ref[zh, 16 * zl + HALF : 16 * zl + 16, :]
            for pair in range(2):
                parts = [rows_ref[zh, pl.ds(32 * pair + b, 8, stride=4), :] for b in range(4)]
                for x, part in enumerate(swap_blocks(parts)):
                    first = 16 * zh + 4 * x + 2 * pair
                    send[first] = part[:4].astype(BF16)
                    send[first + 1] = part[4:].astype(BF16)

    def rows_of(ref, g):
        return jnp.concatenate([ref[g, :, t].reshape(48, LANES) for t in range(TILES)], axis=1)

    def all_rows(ref):
        return jnp.concatenate(
            [
                jnp.concatenate([ref[:, zl, t].reshape(128, LANES) for zl in range(3)], axis=0)
                for t in range(TILES)
            ],
            axis=1,
        )

    pad_ref[...] = jnp.zeros_like(pad_ref)
    slots_ref[...] = jnp.zeros_like(slots_ref)
    loads[0].wait()
    values = padded_transpose(pair_ref)
    centre = values - jnp.mean(values, axis=0, keepdims=True)
    inv_std = lax.rsqrt(jnp.mean(centre * centre, axis=0, keepdims=True) + EPS)
    zhat = centre * inv_std
    normed = zhat.astype(BF16)
    loads[1].wait()
    w_rows = w_proj_ref[...].astype(F32).T.astype(BF16)
    projected = dot(w_rows[128:], normed)
    right_gate = jax.nn.sigmoid(projected[:64])
    right_value = projected[64:]
    to_slots(right_gate * right_value, send_a)

    pl.semaphore_wait(barrier, GROUP - 1 + PEERS - 1)
    exchange(0, send_a, recv_a)

    projected = dot(w_rows[:128], normed)
    left_gate = jax.nn.sigmoid(projected[:64])
    left_value = projected[64:]
    to_slots(left_gate * left_value, send_b)
    exchange(1, send_b, recv_b)

    for load in loads[2:]:
        load.wait()
    w_gate_t = w_gate_ref[...].astype(F32).T.astype(BF16)
    ow_t = ow_ref[...].astype(F32).T.astype(BF16)
    upstream = padded_transpose(d_out_ref)
    gate = jax.nn.sigmoid(dot(w_gate_t, normed))
    d_xhat = dot(ow_ref[...], (upstream * gate).astype(BF16))
    d_xhat_mean = jnp.mean(d_xhat, axis=0, keepdims=True)
    gate_slope = upstream * gate * (1.0 - gate)

    wait_all(recv_a, recv_sem.at[0])
    for t, tile in enumerate(gather_rows(recv_a)):
        right_ref[peer, :, t] = tile.astype(BF16).reshape(3, 16, LANES)
    share(2, lambda to: right_ref.at[peer], right_ref)
    wait_all(recv_b, recv_sem.at[1])
    for t, tile in enumerate(gather_rows(recv_b)):
        left_ref[peer, :, t] = tile.astype(BF16).reshape(3, 16, LANES)
    share(3, lambda to: left_ref.at[peer], left_ref)
    wait_sends(0, send_a)
    wait_sends(1, send_b)
    wait_all(right_ref.at[pl.ds(0, PEERS - 1)], recv_sem.at[2])
    right = all_rows(right_ref)
    scatter_rows(dot_t(rows_of(left_ref, peer), right), send_d)
    exchange(4, send_d, recv_d)
    wait_sends(2, right_ref)
    wait_all(recv_d, recv_sem.at[4])

    x = from_slots(recv_d)
    x_centre = x - jnp.mean(x, axis=0, keepdims=True)
    x_inv = lax.rsqrt(jnp.mean(x_centre * x_centre, axis=0, keepdims=True) + EPS)
    xhat = x_centre * x_inv
    d_x = (d_xhat - d_xhat_mean - xhat * jnp.mean(d_xhat * xhat, axis=0, keepdims=True)) * x_inv
    slots_ref[...] = jnp.zeros_like(slots_ref)
    to_slots(d_x, send_e)
    exchange(5, send_e, recv_e)

    mixed = dot(ow_t, xhat.astype(BF16))
    d_gate = (mixed * gate_slope).astype(BF16)
    d_normed = dot(w_gate_ref[...], d_gate)
    wait_sends(3, left_ref)
    wait_sends(4, send_d)

    wait_all(recv_e, recv_sem.at[5])
    d_x_rows = jnp.concatenate(gather_rows(recv_e), axis=1)
    padded = jnp.concatenate([d_x_rows, jnp.zeros((80, CELLS), F32)], axis=0)
    d_x_cols = padded.T.astype(BF16).reshape(3, PEERS, 16, LANES)
    for to in range(PEERS):
        send_f[to] = d_x_cols[:, to]
    recv_f[peer] = send_f[peer]
    share(6, lambda to: send_f.at[to], recv_f)

    scatter_rows(dot(d_x_rows.astype(BF16), right), send_g)
    exchange(7, send_g, recv_g)
    wait_sends(5, send_e)
    wait_all(left_ref.at[pl.ds(0, PEERS - 1)], recv_sem.at[3])
    wait_all(recv_f.at[pl.ds(0, PEERS - 1)], recv_sem.at[6])
    d_right = None
    for g in range(PEERS):
        term = dot(recv_f[g].reshape(48, LANES)[:, :48], rows_of(left_ref, g))
        d_right = term if d_right is None else d_right + term
    scatter_rows(d_right, send_h)
    exchange(8, send_h, recv_h)

    def back(grad, gates, vals, columns):
        d_vals = grad * gates
        d_gates = d_vals * vals * (1.0 - gates)
        return dot(columns, jnp.concatenate([d_gates.astype(BF16), d_vals.astype(BF16)], axis=0))

    wait_sends(6, send_f)
    wait_all(recv_g, recv_sem.at[7])
    d_normed += back(from_slots(recv_g), left_gate, left_value, w_proj_ref[:, :128])
    wait_sends(7, send_g)
    wait_all(recv_h, recv_sem.at[8])
    d_normed += back(from_slots(recv_h), right_gate, right_value, w_proj_ref[:, 128:])
    grad_mean = jnp.mean(d_normed, axis=0, keepdims=True)
    cross_mean = jnp.mean(d_normed * zhat, axis=0, keepdims=True)
    pad_ref[...] = ((d_normed - grad_mean - zhat * cross_mean) * inv_std).T
    for i in range(TILE_I):
        out_ref[i, :HALF, :] = pad_ref[32 * i : 32 * i + HALF, :]
        out_ref[i, HALF:, :] = pad_ref[32 * i + 16 : 32 * i + 16 + HALF, :]
    wait_sends(8, send_h)


def per_device(pair, d_out, w_proj, w_gate, output_weight):
    slots = pltpu.VMEM((GROUP, 4, LANES), BF16)
    rows = pltpu.VMEM((PEERS, 3, TILES, 16, LANES), BF16)
    blocks = pltpu.VMEM((PEERS, 3, 16, LANES), BF16)
    args = (pair, d_out, w_proj, w_gate, output_weight)
    return pl.pallas_call(
        body,
        out_shape=jax.ShapeDtypeStruct(pair.shape, F32),
        in_specs=[pl.BlockSpec(memory_space=pltpu.HBM)] * 5,
        out_specs=pl.BlockSpec(memory_space=pltpu.VMEM),
        scratch_shapes=[
            *(pltpu.VMEM(a.shape, a.dtype) for a in args),
            pltpu.VMEM((CELLS, LANES), F32),
            pltpu.VMEM((GROUP * 4, LANES), F32),
            pltpu.VMEM((4, 64, LANES), F32),
            rows, rows,
            slots, slots,
            slots, slots,
            slots, slots,
            slots, slots,
            blocks, blocks,
            slots, slots,
            slots, slots,
            pltpu.SemaphoreType.DMA((5,)),
            pltpu.SemaphoreType.DMA((9,)),
            pltpu.SemaphoreType.DMA((9,)),
        ],
        compiler_params=pltpu.CompilerParams(
            collective_id=0, has_side_effects=True, vmem_limit_bytes=60 * 1024 * 1024
        ),
    )(*args)


def solution(mesh):
    return jax.shard_map(
        per_device,
        mesh=mesh,
        in_specs=(P("row", "col", None), P("row", "col", None), P(), P(), P()),
        out_specs=P("row", "col", None),
        check_vma=False,
    )
```

```python
import jax
import jax.numpy as jnp
from jax import lax
from jax.experimental import pallas as pl
from jax.experimental.pallas import tpu as pltpu
from jax.sharding import PartitionSpec as P

EPS = 1e-05
MESH = pl.DeviceIdType.MESH
F32 = jnp.float32
BF16 = jnp.bfloat16

LANES = 128
GROUP = 64
PEERS = 8
HALF = 12
TILE_I = 12
CELLS = 384
TILES = CELLS // LANES


def dot(a, b):
    return lax.dot_general(a, b, (((1,), (0,)), ((), ())), preferred_element_type=F32)


def dot_t(a, b):
    return lax.dot_general(a, b, (((1,), (1,)), ((), ())), preferred_element_type=F32)


def swap_blocks(parts):
    lane = lax.broadcasted_iota(jnp.int32, parts[0].shape, 1)
    low = lane < 64
    even = (lane // 32) % 2 == 0
    p0, p1, p2, p3 = parts
    t0 = jnp.where(low, p0, pltpu.roll(p2, 64, 1))
    t2 = jnp.where(low, pltpu.roll(p0, 64, 1), p2)
    t1 = jnp.where(low, p1, pltpu.roll(p3, 64, 1))
    t3 = jnp.where(low, pltpu.roll(p1, 64, 1), p3)
    u0 = jnp.where(even, t0, pltpu.roll(t1, 32, 1))
    u1 = jnp.where(even, pltpu.roll(t0, 96, 1), t1)
    u2 = jnp.where(even, t2, pltpu.roll(t3, 32, 1))
    u3 = jnp.where(even, pltpu.roll(t2, 96, 1), t3)
    return u0, u1, u2, u3


def close_gaps(tiles):
    place = lax.broadcasted_iota(jnp.int32, tiles[0].shape, 1) % 16
    return [
        jnp.where(place < HALF, tiles[t], pltpu.roll(tiles[3], HALF - 4 * t, 1)) for t in range(3)
    ]


def open_gaps(tiles):
    place = lax.broadcasted_iota(jnp.int32, tiles[0].shape, 1) % 16
    back = [pltpu.roll(tiles[t], LANES - HALF + 4 * t, 1) for t in range(3)]
    return list(tiles) + [jnp.where(place < 4, back[0], jnp.where(place < 8, back[1], back[2]))]


def body(
    pair_hbm, d_out_hbm, w_proj_hbm, w_gate_hbm, ow_hbm, out_ref,
    pair_ref, d_out_ref, w_proj_ref, w_gate_ref, ow_ref,
    pad_ref, slots_ref, rows_ref, left_ref, right_ref,
    send_a, recv_a, send_b, recv_b, send_d, recv_d, send_e, recv_e, send_f, recv_f, send_g, recv_g, send_h, recv_h,
    in_sem, send_sem, recv_sem, across_sem,
):
    r = lax.axis_index("row")
    c = lax.axis_index("col")
    peer = lax.rem(r, PEERS)
    x_me = lax.rem(c, 4)
    z_lo = r // PEERS
    z_me = (c // 4) * 4 + z_lo
    slot = (c // 4) * 16 + x_me * 4 + z_lo
    barrier = pltpu.get_barrier_semaphore()

    def each_of_group(act):
        def at(dz, dx):
            z = lax.rem(z_me + dz, 16)
            x = lax.rem(x_me + dx, 4)
            act((lax.rem(z, 4) * PEERS + peer, (z // 4) * 4 + x), (z // 4) * 16 + x * 4 + lax.rem(z, 4))

        def step(n, carry):
            away = (n + 1) // 2
            dz = 8 + jnp.where(lax.rem(n, 2) == 1, away, -away)
            for dx in (2, 1, 3, 0):
                at(dz, dx)
            return carry

        lax.fori_loop(0, 15, step, 0)
        for dx in (2, 1, 3):
            at(0, dx)

    def each_peer(act):
        def step(d, carry):
            to = lax.rem(peer + d, PEERS)
            act((z_lo * PEERS + to, c), to)
            return carry

        lax.fori_loop(1, PEERS, step, 0)

    def greet(device, _):
        pl.semaphore_signal(barrier, inc=1, device_id=device, device_id_type=MESH)

    each_of_group(greet)
    each_peer(greet)

    loads = [
        pltpu.make_async_copy(src, dst, in_sem.at[n])
        for n, (src, dst) in enumerate((
            (pair_hbm, pair_ref), (w_proj_hbm, w_proj_ref), (d_out_hbm, d_out_ref),
            (w_gate_hbm, w_gate_ref), (ow_hbm, ow_ref),
        ))
    ]
    for load in loads:
        load.start()

    def wait_all(ref, sem):
        pltpu.make_async_copy(ref, ref, sem).wait()

    def exchange(phase, send, recv):
        def one(device, to):
            pltpu.make_async_remote_copy(
                src_ref=send.at[to], dst_ref=recv.at[slot],
                send_sem=send_sem.at[phase], recv_sem=recv_sem.at[phase],
                device_id=device, device_id_type=MESH,
            ).start()

        each_of_group(one)
        pltpu.make_async_copy(send.at[slot], recv.at[slot], recv_sem.at[phase]).start()

    def share(phase, src_of, recv):
        def one(device, to):
            pltpu.make_async_remote_copy(
                src_ref=src_of(to), dst_ref=recv.at[peer],
                send_sem=send_sem.at[phase], recv_sem=recv_sem.at[phase],
                device_id=device, device_id_type=MESH,
            ).start()

        each_peer(one)

    def move_right(block, to, send, recv):
        pltpu.make_async_remote_copy(
            src_ref=right_ref.at[block], dst_ref=right_ref.at[block], send_sem=send, recv_sem=recv,
            device_id=(z_lo * PEERS + to, c), device_id_type=MESH,
        ).start()

    sibling = peer + 1 - 2 * lax.rem(peer, 2)

    def start_across():
        for d in (2, 1, 3):
            move_right(peer, lax.rem(peer + 2 * d, PEERS), send_sem.at[2], across_sem.at[d])
        move_right(peer, sibling, send_sem.at[9], recv_sem.at[2])

    def to_sibling():
        for d in (1, 3, 2):
            block = lax.rem(peer + PEERS - 2 * d, PEERS)
            wait_all(right_ref.at[block], across_sem.at[d])
            move_right(block, sibling, send_sem.at[9], recv_sem.at[2])

    def wait_sends(phase, ref):
        wait_all(ref.at[pl.ds(0, ref.shape[0] - 1)], send_sem.at[phase])

    def padded_transpose(ref):
        for i in range(TILE_I):
            cells = ref[i].astype(F32)
            pad_ref[32 * i : 32 * i + HALF, :] = cells[:HALF]
            pad_ref[32 * i + 16 : 32 * i + 16 + HALF, :] = cells[HALF:]
        return pad_ref[...].T

    def tile_of(array, t):
        return array[:, LANES * t : LANES * (t + 1)]

    def to_slots(array, send):
        for a in range(TILES):
            slots_ref[pl.ds(a, GROUP, stride=4), :] = tile_of(array, a)
        for n in range(GROUP):
            send[n] = slots_ref[4 * n : 4 * n + 4, :].astype(BF16)

    def from_slots(recv):
        for n in range(GROUP):
            slots_ref[4 * n : 4 * n + 4, :] = recv[n].astype(F32)
        return jnp.concatenate([slots_ref[pl.ds(a, GROUP, stride=4), :] for a in range(TILES)], axis=1)

    def gather_rows(recv):
        for zh in range(4):
            for pair in range(2):
                parts = []
                for x in range(4):
                    first = 16 * zh + 4 * x + 2 * pair
                    parts.append(jnp.concatenate([recv[first].astype(F32), recv[first + 1].astype(F32)], axis=0))
                for b, part in enumerate(swap_blocks(parts)):
                    rows_ref[zh, pl.ds(32 * pair + b, 8, stride=4), :] = part
            for zl in range(3):
                rows_ref[zh, 16 * zl + HALF : 16 * zl + 16, :] = rows_ref[zh, 48 + 4 * zl : 52 + 4 * zl, :]
        return close_gaps([rows_ref[zh, :48, :] for zh in range(4)])

    def scatter_rows(array, send):
        for zh, tile in enumerate(open_gaps([tile_of(array, t) for t in range(TILES)])):
            rows_ref[zh, :48, :] = tile
            for zl in range(3):
                rows_ref[zh, 48 + 4 * zl : 52 + 4 * zl, :] = rows_ref[zh, 16 * zl + HALF : 16 * zl + 16, :]
            for pair in range(2):
                parts = [rows_ref[zh, pl.ds(32 * pair + b, 8, stride=4), :] for b in range(4)]
                for x, part in enumerate(swap_blocks(parts)):
                    first = 16 * zh + 4 * x + 2 * pair
                    send[first] = part[:4].astype(BF16)
                    send[first + 1] = part[4:].astype(BF16)

    def rows_of(ref, g):
        return jnp.concatenate([ref[g, :, t].reshape(48, LANES) for t in range(TILES)], axis=1)

    def all_rows(ref):
        return jnp.concatenate(
            [
                jnp.concatenate([ref[:, zl, t].reshape(128, LANES) for zl in range(3)], axis=0)
                for t in range(TILES)
            ],
            axis=1,
        )

    pad_ref[...] = jnp.zeros_like(pad_ref)
    slots_ref[...] = jnp.zeros_like(slots_ref)
    loads[0].wait()
    values = padded_transpose(pair_ref)
    centre = values - jnp.mean(values, axis=0, keepdims=True)
    inv_std = lax.rsqrt(jnp.mean(centre * centre, axis=0, keepdims=True) + EPS)
    zhat = centre * inv_std
    normed = zhat.astype(BF16)
    loads[1].wait()
    w_rows = w_proj_ref[...].astype(F32).T.astype(BF16)
    projected = dot(w_rows[128:], normed)
    right_gate = jax.nn.sigmoid(projected[:64])
    right_value = projected[64:]
    to_slots(right_gate * right_value, send_a)

    pl.semaphore_wait(barrier, GROUP - 1 + PEERS - 1)
    exchange(0, send_a, recv_a)

    projected = dot(w_rows[:128], normed)
    left_gate = jax.nn.sigmoid(projected[:64])
    left_value = projected[64:]
    to_slots(left_gate * left_value, send_b)
    exchange(1, send_b, recv_b)

    for load in loads[2:]:
        load.wait()
    w_gate_t = w_gate_ref[...].astype(F32).T.astype(BF16)
    ow_t = ow_ref[...].astype(F32).T.astype(BF16)
    upstream = padded_transpose(d_out_ref)
    gate = jax.nn.sigmoid(dot(w_gate_t, normed))
    d_xhat = dot(ow_ref[...], (upstream * gate).astype(BF16))
    d_xhat_mean = jnp.mean(d_xhat, axis=0, keepdims=True)
    gate_slope = upstream * gate * (1.0 - gate)

    wait_all(recv_a, recv_sem.at[0])
    for t, tile in enumerate(gather_rows(recv_a)):
        right_ref[peer, :, t] = tile.astype(BF16).reshape(3, 16, LANES)
    start_across()
    wait_all(recv_b, recv_sem.at[1])
    for t, tile in enumerate(gather_rows(recv_b)):
        left_ref[peer, :, t] = tile.astype(BF16).reshape(3, 16, LANES)
    to_sibling()
    wait_sends(0, send_a)
    wait_sends(1, send_b)
    wait_all(right_ref.at[pl.ds(0, 4)], recv_sem.at[2])
    right = all_rows(right_ref)
    scatter_rows(dot_t(rows_of(left_ref, peer), right), send_d)
    exchange(4, send_d, recv_d)
    share(3, lambda to: left_ref.at[peer], left_ref)
    wait_all(right_ref.at[pl.ds(0, 3)], send_sem.at[2])
    wait_all(right_ref.at[pl.ds(0, 4)], send_sem.at[9])
    wait_all(recv_d, recv_sem.at[4])

    x = from_slots(recv_d)
    x_centre = x - jnp.mean(x, axis=0, keepdims=True)
    x_inv = lax.rsqrt(jnp.mean(x_centre * x_centre, axis=0, keepdims=True) + EPS)
    xhat = x_centre * x_inv
    d_x = (d_xhat - d_xhat_mean - xhat * jnp.mean(d_xhat * xhat, axis=0, keepdims=True)) * x_inv
    slots_ref[...] = jnp.zeros_like(slots_ref)
    to_slots(d_x, send_e)
    exchange(5, send_e, recv_e)

    mixed = dot(ow_t, xhat.astype(BF16))
    d_gate = (mixed * gate_slope).astype(BF16)
    d_normed = dot(w_gate_ref[...], d_gate)
    wait_sends(3, left_ref)
    wait_sends(4, send_d)

    wait_all(recv_e, recv_sem.at[5])
    d_x_rows = jnp.concatenate(gather_rows(recv_e), axis=1)
    padded = jnp.concatenate([d_x_rows, jnp.zeros((80, CELLS), F32)], axis=0)
    d_x_cols = padded.T.astype(BF16).reshape(3, PEERS, 16, LANES)
    for to in range(PEERS):
        send_f[to] = d_x_cols[:, to]
    recv_f[peer] = send_f[peer]
    share(6, lambda to: send_f.at[to], recv_f)

    scatter_rows(dot(d_x_rows.astype(BF16), right), send_g)
    exchange(7, send_g, recv_g)
    wait_sends(5, send_e)
    wait_all(left_ref.at[pl.ds(0, PEERS - 1)], recv_sem.at[3])
    wait_all(recv_f.at[pl.ds(0, PEERS - 1)], recv_sem.at[6])
    d_right = None
    for g in range(PEERS):
        term = dot(recv_f[g].reshape(48, LANES)[:, :48], rows_of(left_ref, g))
        d_right = term if d_right is None else d_right + term
    scatter_rows(d_right, send_h)
    exchange(8, send_h, recv_h)

    def back(grad, gates, vals, columns):
        d_vals = grad * gates
        d_gates = d_vals * vals * (1.0 - gates)
        return dot(columns, jnp.concatenate([d_gates.astype(BF16), d_vals.astype(BF16)], axis=0))

    wait_sends(6, send_f)
    wait_all(recv_g, recv_sem.at[7])
    d_normed += back(from_slots(recv_g), left_gate, left_value, w_proj_ref[:, :128])
    wait_sends(7, send_g)
    wait_all(recv_h, recv_sem.at[8])
    d_normed += back(from_slots(recv_h), right_gate, right_value, w_proj_ref[:, 128:])
    grad_mean = jnp.mean(d_normed, axis=0, keepdims=True)
    cross_mean = jnp.mean(d_normed * zhat, axis=0, keepdims=True)
    pad_ref[...] = ((d_normed - grad_mean - zhat * cross_mean) * inv_std).T
    for i in range(TILE_I):
        out_ref[i, :HALF, :] = pad_ref[32 * i : 32 * i + HALF, :]
        out_ref[i, HALF:, :] = pad_ref[32 * i + 16 : 32 * i + 16 + HALF, :]
    wait_sends(8, send_h)


def per_device(pair, d_out, w_proj, w_gate, output_weight):
    slots = pltpu.VMEM((GROUP, 4, LANES), BF16)
    rows = pltpu.VMEM((PEERS, 3, TILES, 16, LANES), BF16)
    blocks = pltpu.VMEM((PEERS, 3, 16, LANES), BF16)
    args = (pair, d_out, w_proj, w_gate, output_weight)
    return pl.pallas_call(
        body,
        out_shape=jax.ShapeDtypeStruct(pair.shape, F32),
        in_specs=[pl.BlockSpec(memory_space=pltpu.HBM)] * 5,
        out_specs=pl.BlockSpec(memory_space=pltpu.VMEM),
        scratch_shapes=[
            *(pltpu.VMEM(a.shape, a.dtype) for a in args),
            pltpu.VMEM((CELLS, LANES), F32),
            pltpu.VMEM((GROUP * 4, LANES), F32),
            pltpu.VMEM((4, 64, LANES), F32),
            rows, rows,
            slots, slots,
            slots, slots,
            slots, slots,
            slots, slots,
            blocks, blocks,
            slots, slots,
            slots, slots,
            pltpu.SemaphoreType.DMA((5,)),
            pltpu.SemaphoreType.DMA((10,)),
            pltpu.SemaphoreType.DMA((9,)),
            pltpu.SemaphoreType.DMA((4,)),
        ],
        compiler_params=pltpu.CompilerParams(
            collective_id=0, has_side_effects=True, vmem_limit_bytes=48 * 1024 * 1024
        ),
    )(*(pltpu.with_memory_space_constraint(a, pltpu.HBM) for a in args))


def solution(mesh):
    return jax.shard_map(
        per_device,
        mesh=mesh,
        in_specs=(P("row", "col", None), P("row", "col", None), P(), P(), P()),
        out_specs=P("row", "col", None),
        check_vma=False,
    )
```

```python
import jax
import jax.numpy as jnp
from jax import lax
from jax.experimental import pallas as pl
from jax.experimental.pallas import tpu as pltpu
from jax.sharding import PartitionSpec as P

EPS = 1e-05
MESH = pl.DeviceIdType.MESH
F32 = jnp.float32
BF16 = jnp.bfloat16

LANES = 128
GROUP = 64
PEERS = 8
HALF = 12
TILE_I = 12
CELLS = 384
TILES = CELLS // LANES


def dot(a, b):
    return lax.dot_general(a, b, (((1,), (0,)), ((), ())), preferred_element_type=F32)


def dot_t(a, b):
    return lax.dot_general(a, b, (((1,), (1,)), ((), ())), preferred_element_type=F32)


def swap_blocks(parts):
    lane = lax.broadcasted_iota(jnp.int32, parts[0].shape, 1)
    low = lane < 64
    even = (lane // 32) % 2 == 0
    p0, p1, p2, p3 = parts
    t0 = jnp.where(low, p0, pltpu.roll(p2, 64, 1))
    t2 = jnp.where(low, pltpu.roll(p0, 64, 1), p2)
    t1 = jnp.where(low, p1, pltpu.roll(p3, 64, 1))
    t3 = jnp.where(low, pltpu.roll(p1, 64, 1), p3)
    u0 = jnp.where(even, t0, pltpu.roll(t1, 32, 1))
    u1 = jnp.where(even, pltpu.roll(t0, 96, 1), t1)
    u2 = jnp.where(even, t2, pltpu.roll(t3, 32, 1))
    u3 = jnp.where(even, pltpu.roll(t2, 96, 1), t3)
    return u0, u1, u2, u3


def close_gaps(tiles):
    place = lax.broadcasted_iota(jnp.int32, tiles[0].shape, 1) % 16
    return [
        jnp.where(place < HALF, tiles[t], pltpu.roll(tiles[3], HALF - 4 * t, 1)) for t in range(3)
    ]


def open_gaps(tiles):
    place = lax.broadcasted_iota(jnp.int32, tiles[0].shape, 1) % 16
    back = [pltpu.roll(tiles[t], LANES - HALF + 4 * t, 1) for t in range(3)]
    return list(tiles) + [jnp.where(place < 4, back[0], jnp.where(place < 8, back[1], back[2]))]


def body(
    pair_hbm, d_out_hbm, w_proj_hbm, w_gate_hbm, ow_hbm, out_ref,
    pair_ref, d_out_ref, w_proj_ref, w_gate_ref, ow_ref,
    pad_ref, slots_ref, rows_ref, left_ref, right_ref,
    send_a, recv_a, send_b, recv_b, send_d, recv_d, send_e, recv_e, send_f, recv_f, send_g, recv_g, send_h, recv_h,
    in_sem, send_sem, recv_sem, right_sem, across_sem,
):
    r = lax.axis_index("row")
    c = lax.axis_index("col")
    peer = lax.rem(r, PEERS)
    x_me = lax.rem(c, 4)
    z_lo = r // PEERS
    z_hi = c // 4
    z_me = z_hi * 4 + z_lo
    slot = (c // 4) * 16 + x_me * 4 + z_lo
    order_x = [lax.rem(x_me + dx, 4) for dx in (2, 1, 3, 0)]
    barrier = pltpu.get_barrier_semaphore()

    def each_of_group(act):
        def plane(dz, columns):
            z = lax.rem(z_me + dz, 16)
            high = lax.div(z, 4)
            low = z - 4 * high
            row = low * PEERS + peer
            col = high * 4
            base = high * 16 + low
            for x in columns:
                act((row, col + x), base + 4 * x)

        def step(n, carry):
            away = lax.div(n + 1, 2)
            plane(8 + jnp.where(lax.rem(n, 2) == 1, away, -away), order_x)
            return carry

        lax.fori_loop(0, 15, step, 0)
        plane(0, order_x[:3])

    def each_peer(act):
        def step(d, carry):
            to = lax.rem(peer + d, PEERS)
            act((z_lo * PEERS + to, c), to)
            return carry

        lax.fori_loop(1, PEERS, step, 0)

    loads = [
        pltpu.make_async_copy(src, dst, in_sem.at[n])
        for n, (src, dst) in enumerate((
            (pair_hbm, pair_ref), (w_proj_hbm, w_proj_ref), (d_out_hbm, d_out_ref),
            (w_gate_hbm, w_gate_ref), (ow_hbm, ow_ref),
        ))
    ]
    for load in loads:
        load.start()

    def greet(device, _):
        pl.semaphore_signal(barrier, inc=1, device_id=device, device_id_type=MESH)

    each_of_group(greet)
    each_peer(greet)

    def wait_all(ref, sem):
        pltpu.make_async_copy(ref, ref, sem).wait()

    def exchange(phase, send, recv):
        def one(device, to):
            pltpu.make_async_remote_copy(
                src_ref=send.at[to], dst_ref=recv.at[slot],
                send_sem=send_sem.at[phase], recv_sem=recv_sem.at[phase],
                device_id=device, device_id_type=MESH,
            ).start()

        each_of_group(one)
        pltpu.make_async_copy(send.at[slot], recv.at[slot], recv_sem.at[phase]).start()

    def exchange_right():
        def one(device, to):
            opposite = jnp.where(lax.rem(to // 16 + 4 - z_hi, 4) == 2, 1, 0)
            pltpu.make_async_remote_copy(
                src_ref=send_a.at[to], dst_ref=recv_a.at[slot],
                send_sem=send_sem.at[0], recv_sem=right_sem.at[opposite],
                device_id=device, device_id_type=MESH,
            ).start()

        each_of_group(one)
        pltpu.make_async_copy(send_a.at[slot], recv_a.at[slot], right_sem.at[0]).start()

    def share(phase, src_of, recv):
        def one(device, to):
            pltpu.make_async_remote_copy(
                src_ref=src_of(to), dst_ref=recv.at[peer],
                send_sem=send_sem.at[phase], recv_sem=recv_sem.at[phase],
                device_id=device, device_id_type=MESH,
            ).start()

        each_peer(one)

    sibling = peer + 1 - 2 * lax.rem(peer, 2)
    nearer = [lax.rem(z_hi + away, 4) for away in (0, 1, 3)]
    opposite = lax.rem(z_hi + 2, 4)

    def move_right(block, zh, to, send, recv):
        pltpu.make_async_remote_copy(
            src_ref=right_ref.at[block, zh], dst_ref=right_ref.at[block, zh], send_sem=send, recv_sem=recv,
            device_id=(z_lo * PEERS + to, c), device_id_type=MESH,
        ).start()

    def start_across(parts, part):
        for d in (2, 1, 3):
            for zh in parts:
                move_right(peer, zh, lax.rem(peer + 2 * d, PEERS), send_sem.at[2], across_sem.at[d, part])
        for zh in parts:
            move_right(peer, zh, sibling, send_sem.at[9], recv_sem.at[2])

    def to_sibling(parts, part):
        for d in (1, 3, 2):
            block = lax.rem(peer + PEERS - 2 * d, PEERS)
            wait_all(right_ref.at[block, pl.ds(0, len(parts))], across_sem.at[d, part])
            for zh in parts:
                move_right(block, zh, sibling, send_sem.at[9], recv_sem.at[2])

    def wait_sends(phase, ref):
        wait_all(ref.at[pl.ds(0, ref.shape[0] - 1)], send_sem.at[phase])

    def padded_transpose(ref):
        for i in range(TILE_I):
            cells = ref[i].astype(F32)
            pad_ref[32 * i : 32 * i + HALF, :] = cells[:HALF]
            pad_ref[32 * i + 16 : 32 * i + 16 + HALF, :] = cells[HALF:]
        return pad_ref[...].T

    def tile_of(array, t):
        return array[:, LANES * t : LANES * (t + 1)]

    def to_slots(array, send):
        for a in range(TILES):
            slots_ref[pl.ds(a, GROUP, stride=4), :] = tile_of(array, a)
        for n in range(GROUP):
            send[n] = slots_ref[4 * n : 4 * n + 4, :].astype(BF16)

    def from_slots(recv):
        for n in range(GROUP):
            slots_ref[4 * n : 4 * n + 4, :] = recv[n].astype(F32)
        return jnp.concatenate([slots_ref[pl.ds(a, GROUP, stride=4), :] for a in range(TILES)], axis=1)

    def gather_block(recv, zh):
        for pair in range(2):
            parts = []
            for x in range(4):
                first = 16 * zh + 4 * x + 2 * pair
                parts.append(jnp.concatenate([recv[first].astype(F32), recv[first + 1].astype(F32)], axis=0))
            for b, part in enumerate(swap_blocks(parts)):
                rows_ref[zh, pl.ds(32 * pair + b, 8, stride=4), :] = part
        for zl in range(3):
            rows_ref[zh, 16 * zl + HALF : 16 * zl + 16, :] = rows_ref[zh, 48 + 4 * zl : 52 + 4 * zl, :]

    def keep_block(recv, zh, ref):
        gather_block(recv, zh)
        ref[peer, zh] = rows_ref[zh, :48, :].astype(BF16).reshape(3, 16, LANES)

    def scatter_rows(tiles, send):
        for zh, tile in enumerate(tiles):
            rows_ref[zh, :48, :] = tile
            for zl in range(3):
                rows_ref[zh, 48 + 4 * zl : 52 + 4 * zl, :] = rows_ref[zh, 16 * zl + HALF : 16 * zl + 16, :]
            for pair in range(2):
                parts = [rows_ref[zh, pl.ds(32 * pair + b, 8, stride=4), :] for b in range(4)]
                for x, part in enumerate(swap_blocks(parts)):
                    first = 16 * zh + 4 * x + 2 * pair
                    send[first] = part[:4].astype(BF16)
                    send[first + 1] = part[4:].astype(BF16)

    def tiles_of(array):
        return [tile_of(array, t) for t in range(array.shape[1] // LANES)]

    def rows_of(ref, g):
        return jnp.concatenate([ref[g, zh].reshape(48, LANES) for zh in range(4)], axis=1)

    def all_rows(ref):
        return jnp.concatenate(
            [
                jnp.concatenate([ref[:, zh, zl].reshape(128, LANES) for zl in range(3)], axis=0)
                for zh in range(4)
            ],
            axis=1,
        )

    pad_ref[...] = jnp.zeros_like(pad_ref)
    slots_ref[...] = jnp.zeros_like(slots_ref)
    loads[0].wait()
    values = padded_transpose(pair_ref)
    centre = values - jnp.mean(values, axis=0, keepdims=True)
    inv_std = lax.rsqrt(jnp.mean(centre * centre, axis=0, keepdims=True) + EPS)
    zhat = centre * inv_std
    normed = zhat.astype(BF16)
    loads[1].wait()
    w_rows = w_proj_ref[...].astype(F32).T.astype(BF16)
    projected = dot(w_rows[128:], normed)
    right_gate = jax.nn.sigmoid(projected[:64])
    right_value = projected[64:]
    to_slots(right_gate * right_value, send_a)

    pl.semaphore_wait(barrier, GROUP - 1 + PEERS - 1)
    exchange_right()

    projected = dot(w_rows[:128], normed)
    left_gate = jax.nn.sigmoid(projected[:64])
    left_value = projected[64:]
    to_slots(left_gate * left_value, send_b)
    exchange(1, send_b, recv_b)

    for load in loads[2:]:
        load.wait()
    w_gate_t = w_gate_ref[...].astype(F32).T.astype(BF16)
    ow_t = ow_ref[...].astype(F32).T.astype(BF16)
    upstream = padded_transpose(d_out_ref)
    gate = jax.nn.sigmoid(dot(w_gate_t, normed))
    d_xhat = dot(ow_ref[...], (upstream * gate).astype(BF16))
    d_xhat_mean = jnp.mean(d_xhat, axis=0, keepdims=True)
    gate_slope = upstream * gate * (1.0 - gate)

    wait_all(recv_a.at[pl.ds(0, 48)], right_sem.at[0])
    for zh in nearer:
        keep_block(recv_a, zh, right_ref)
    start_across(nearer, 0)
    wait_all(recv_a.at[pl.ds(0, 16)], right_sem.at[1])
    keep_block(recv_a, opposite, right_ref)
    start_across([opposite], 1)
    to_sibling(nearer, 0)
    wait_all(recv_b, recv_sem.at[1])
    for zh in range(4):
        keep_block(recv_b, zh, left_ref)
    to_sibling([opposite], 1)
    wait_sends(0, send_a)
    wait_sends(1, send_b)
    wait_all(right_ref.at[pl.ds(0, 4)], recv_sem.at[2])
    right = all_rows(right_ref)
    scatter_rows(open_gaps(tiles_of(dot_t(rows_of(left_ref, peer), right))), send_d)
    exchange(4, send_d, recv_d)
    share(3, lambda to: left_ref.at[peer], left_ref)
    wait_all(right_ref.at[pl.ds(0, 3)], send_sem.at[2])
    wait_all(right_ref.at[pl.ds(0, 4)], send_sem.at[9])
    wait_all(recv_d, recv_sem.at[4])

    x = from_slots(recv_d)
    x_centre = x - jnp.mean(x, axis=0, keepdims=True)
    x_inv = lax.rsqrt(jnp.mean(x_centre * x_centre, axis=0, keepdims=True) + EPS)
    xhat = x_centre * x_inv
    d_x = (d_xhat - d_xhat_mean - xhat * jnp.mean(d_xhat * xhat, axis=0, keepdims=True)) * x_inv
    to_slots(d_x, send_e)
    exchange(5, send_e, recv_e)

    mixed = dot(ow_t, xhat.astype(BF16))
    d_gate = (mixed * gate_slope).astype(BF16)
    d_normed = dot(w_gate_ref[...], d_gate)
    wait_sends(3, left_ref)
    wait_sends(4, send_d)

    wait_all(recv_e, recv_sem.at[5])
    for zh in range(4):
        gather_block(recv_e, zh)
    d_x_rows = jnp.concatenate(close_gaps([rows_ref[zh, :48, :] for zh in range(4)]), axis=1)
    padded = jnp.concatenate([d_x_rows, jnp.zeros((80, CELLS), F32)], axis=0)
    d_x_cols = padded.T.astype(BF16).reshape(3, PEERS, 16, LANES)
    for to in range(PEERS):
        send_f[to] = d_x_cols[:, to]
    recv_f[peer] = send_f[peer]
    share(6, lambda to: send_f.at[to], recv_f)

    scatter_rows(tiles_of(dot(d_x_rows.astype(BF16), right)), send_g)
    exchange(7, send_g, recv_g)
    wait_sends(5, send_e)
    wait_all(left_ref.at[pl.ds(0, PEERS - 1)], recv_sem.at[3])
    wait_all(recv_f.at[pl.ds(0, PEERS - 1)], recv_sem.at[6])
    d_right = None
    for g in range(PEERS):
        term = dot(recv_f[g].reshape(48, LANES)[:, :48], rows_of(left_ref, g))
        d_right = term if d_right is None else d_right + term
    scatter_rows(tiles_of(d_right), send_h)
    exchange(8, send_h, recv_h)

    def back(grad, gates, vals, columns):
        d_vals = grad * gates
        d_gates = d_vals * vals * (1.0 - gates)
        return dot(columns, jnp.concatenate([d_gates.astype(BF16), d_vals.astype(BF16)], axis=0))

    wait_sends(6, send_f)
    wait_all(recv_g, recv_sem.at[7])
    d_normed += back(from_slots(recv_g), left_gate, left_value, w_proj_ref[:, :128])
    wait_sends(7, send_g)
    wait_all(recv_h, recv_sem.at[8])
    d_normed += back(from_slots(recv_h), right_gate, right_value, w_proj_ref[:, 128:])
    grad_mean = jnp.mean(d_normed, axis=0, keepdims=True)
    cross_mean = jnp.mean(d_normed * zhat, axis=0, keepdims=True)
    d_pair = ((d_normed - grad_mean - zhat * cross_mean) * inv_std).T
    for i in range(TILE_I):
        out_ref[i, :HALF, :] = d_pair[32 * i : 32 * i + HALF]
        out_ref[i, HALF:, :] = d_pair[32 * i + 16 : 32 * i + 16 + HALF]
    wait_sends(8, send_h)


def per_device(pair, d_out, w_proj, w_gate, output_weight):
    slots = pltpu.VMEM((GROUP, 4, LANES), BF16)
    rows = pltpu.VMEM((PEERS, 4, 3, 16, LANES), BF16)
    blocks = pltpu.VMEM((PEERS, 3, 16, LANES), BF16)
    args = (pair, d_out, w_proj, w_gate, output_weight)
    return pl.pallas_call(
        body,
        out_shape=jax.ShapeDtypeStruct(pair.shape, F32),
        in_specs=[pl.BlockSpec(memory_space=pltpu.HBM)] * 5,
        out_specs=pl.BlockSpec(memory_space=pltpu.VMEM),
        scratch_shapes=[
            *(pltpu.VMEM(a.shape, a.dtype) for a in args),
            pltpu.VMEM((CELLS, LANES), F32),
            pltpu.VMEM((GROUP * 4, LANES), F32),
            pltpu.VMEM((4, 64, LANES), F32),
            rows, rows,
            slots, slots,
            slots, slots,
            slots, slots,
            slots, slots,
            blocks, blocks,
            slots, slots,
            slots, slots,
            pltpu.SemaphoreType.DMA((5,)),
            pltpu.SemaphoreType.DMA((10,)),
            pltpu.SemaphoreType.DMA((9,)),
            pltpu.SemaphoreType.DMA((2,)),
            pltpu.SemaphoreType.DMA((4, 2)),
        ],
        compiler_params=pltpu.CompilerParams(
            collective_id=0, has_side_effects=True, vmem_limit_bytes=48 * 1024 * 1024
        ),
    )(*(pltpu.with_memory_space_constraint(a, pltpu.HBM) for a in args))


def solution(mesh):
    return jax.shard_map(
        per_device,
        mesh=mesh,
        in_specs=(P("row", "col", None), P("row", "col", None), P(), P(), P()),
        out_specs=P("row", "col", None),
        check_vma=False,
    )
```

```python
import jax
import jax.numpy as jnp
from jax import lax
from jax.experimental import pallas as pl
from jax.experimental.pallas import tpu as pltpu
from jax.sharding import PartitionSpec as P

EPS = 1e-05
MESH = pl.DeviceIdType.MESH
F32 = jnp.float32
BF16 = jnp.bfloat16

LANES = 128
GROUP = 64
PEERS = 8
HALF = 12
TILE_I = 12
CELLS = 384
TILES = CELLS // LANES


def dot(a, b):
    return lax.dot_general(a, b, (((1,), (0,)), ((), ())), preferred_element_type=F32)


def dot_t(a, b):
    return lax.dot_general(a, b, (((1,), (1,)), ((), ())), preferred_element_type=F32)


def swap_blocks(parts):
    lane = lax.broadcasted_iota(jnp.int32, parts[0].shape, 1)
    low = lane < 64
    even = (lane // 32) % 2 == 0
    p0, p1, p2, p3 = parts
    t0 = jnp.where(low, p0, pltpu.roll(p2, 64, 1))
    t2 = jnp.where(low, pltpu.roll(p0, 64, 1), p2)
    t1 = jnp.where(low, p1, pltpu.roll(p3, 64, 1))
    t3 = jnp.where(low, pltpu.roll(p1, 64, 1), p3)
    u0 = jnp.where(even, t0, pltpu.roll(t1, 32, 1))
    u1 = jnp.where(even, pltpu.roll(t0, 96, 1), t1)
    u2 = jnp.where(even, t2, pltpu.roll(t3, 32, 1))
    u3 = jnp.where(even, pltpu.roll(t2, 96, 1), t3)
    return u0, u1, u2, u3


def close_gaps(tiles):
    place = lax.broadcasted_iota(jnp.int32, tiles[0].shape, 1) % 16
    return [
        jnp.where(place < HALF, tiles[t], pltpu.roll(tiles[3], HALF - 4 * t, 1)) for t in range(3)
    ]


def open_gaps(tiles):
    place = lax.broadcasted_iota(jnp.int32, tiles[0].shape, 1) % 16
    back = [pltpu.roll(tiles[t], LANES - HALF + 4 * t, 1) for t in range(3)]
    return list(tiles) + [jnp.where(place < 4, back[0], jnp.where(place < 8, back[1], back[2]))]


def body(
    pair_hbm, d_out_hbm, w_proj_hbm, w_gate_hbm, ow_hbm, out_ref,
    pair_ref, d_out_ref, w_proj_ref, w_gate_ref, ow_ref,
    pad_ref, slots_ref, rows_ref, left_ref, right_ref,
    send_a, recv_a, send_b, recv_b, send_d, recv_d, send_e, recv_e, send_f, recv_f, send_g, recv_g, send_h, recv_h,
    in_sem, send_sem, recv_sem, right_sem, d_x_sem, across_sem,
):
    r = lax.axis_index("row")
    c = lax.axis_index("col")
    peer = lax.rem(r, PEERS)
    x_me = lax.rem(c, 4)
    z_lo = r // PEERS
    z_hi = c // 4
    z_me = z_hi * 4 + z_lo
    slot = (c // 4) * 16 + x_me * 4 + z_lo
    order_x = [lax.rem(x_me + dx, 4) for dx in (2, 1, 3, 0)]
    barrier = pltpu.get_barrier_semaphore()

    def each_of_group(act):
        def plane(dz, columns):
            z = lax.rem(z_me + dz, 16)
            high = lax.div(z, 4)
            low = z - 4 * high
            row = low * PEERS + peer
            col = high * 4
            base = high * 16 + low
            for x in columns:
                act((row, col + x), base + 4 * x)

        def step(n, carry):
            away = lax.div(n + 1, 2)
            plane(8 + jnp.where(lax.rem(n, 2) == 1, away, -away), order_x)
            return carry

        lax.fori_loop(0, 15, step, 0)
        plane(0, order_x[:3])

    def each_peer(act):
        def step(d, carry):
            to = lax.rem(peer + d, PEERS)
            act((z_lo * PEERS + to, c), to)
            return carry

        lax.fori_loop(1, PEERS, step, 0)

    loads = [
        pltpu.make_async_copy(src, dst, in_sem.at[n])
        for n, (src, dst) in enumerate((
            (pair_hbm, pair_ref), (w_proj_hbm, w_proj_ref), (d_out_hbm, d_out_ref),
            (w_gate_hbm, w_gate_ref), (ow_hbm, ow_ref),
        ))
    ]
    for load in loads:
        load.start()

    def greet(device, _):
        pl.semaphore_signal(barrier, inc=1, device_id=device, device_id_type=MESH)

    each_of_group(greet)
    each_peer(greet)

    def wait_all(ref, sem):
        pltpu.make_async_copy(ref, ref, sem).wait()

    def exchange(phase, send, recv):
        def one(device, to):
            pltpu.make_async_remote_copy(
                src_ref=send.at[to], dst_ref=recv.at[slot],
                send_sem=send_sem.at[phase], recv_sem=recv_sem.at[phase],
                device_id=device, device_id_type=MESH,
            ).start()

        each_of_group(one)
        pltpu.make_async_copy(send.at[slot], recv.at[slot], recv_sem.at[phase]).start()

    def exchange_split(phase, send, recv, sem):
        def one(device, to):
            opposite = jnp.where(lax.rem(to // 16 + 4 - z_hi, 4) == 2, 1, 0)
            pltpu.make_async_remote_copy(
                src_ref=send.at[to], dst_ref=recv.at[slot],
                send_sem=send_sem.at[phase], recv_sem=sem.at[opposite],
                device_id=device, device_id_type=MESH,
            ).start()

        each_of_group(one)
        pltpu.make_async_copy(send.at[slot], recv.at[slot], sem.at[0]).start()

    def share(phase, src_of, recv):
        def one(device, to):
            pltpu.make_async_remote_copy(
                src_ref=src_of(to), dst_ref=recv.at[peer],
                send_sem=send_sem.at[phase], recv_sem=recv_sem.at[phase],
                device_id=device, device_id_type=MESH,
            ).start()

        each_peer(one)

    sibling = peer + 1 - 2 * lax.rem(peer, 2)
    nearer = [lax.rem(z_hi + away, 4) for away in (0, 1, 3)]
    opposite = lax.rem(z_hi + 2, 4)

    def move_right(block, zh, to, send, recv):
        pltpu.make_async_remote_copy(
            src_ref=right_ref.at[block, zh], dst_ref=right_ref.at[block, zh], send_sem=send, recv_sem=recv,
            device_id=(z_lo * PEERS + to, c), device_id_type=MESH,
        ).start()

    def start_across(parts, part):
        for d in (2, 1, 3):
            for zh in parts:
                move_right(peer, zh, lax.rem(peer + 2 * d, PEERS), send_sem.at[2], across_sem.at[d, part])
        for zh in parts:
            move_right(peer, zh, sibling, send_sem.at[9], recv_sem.at[2])

    def to_sibling(parts, part):
        for d in (1, 3, 2):
            block = lax.rem(peer + PEERS - 2 * d, PEERS)
            wait_all(right_ref.at[block, pl.ds(0, len(parts))], across_sem.at[d, part])
            for zh in parts:
                move_right(block, zh, sibling, send_sem.at[9], recv_sem.at[2])

    def wait_sends(phase, ref):
        wait_all(ref.at[pl.ds(0, ref.shape[0] - 1)], send_sem.at[phase])

    def padded_transpose(ref):
        for i in range(TILE_I):
            cells = ref[i].astype(F32)
            pad_ref[32 * i : 32 * i + HALF, :] = cells[:HALF]
            pad_ref[32 * i + 16 : 32 * i + 16 + HALF, :] = cells[HALF:]
        return pad_ref[...].T

    def tile_of(array, t):
        return array[:, LANES * t : LANES * (t + 1)]

    def to_slots(array, send):
        for a in range(TILES):
            slots_ref[pl.ds(a, GROUP, stride=4), :] = tile_of(array, a)
        for n in range(GROUP):
            send[n] = slots_ref[4 * n : 4 * n + 4, :].astype(BF16)

    def from_slots(recv):
        for n in range(GROUP):
            slots_ref[4 * n : 4 * n + 4, :] = recv[n].astype(F32)
        return jnp.concatenate([slots_ref[pl.ds(a, GROUP, stride=4), :] for a in range(TILES)], axis=1)

    def gather_block(recv, zh):
        for pair in range(2):
            parts = []
            for x in range(4):
                first = 16 * zh + 4 * x + 2 * pair
                parts.append(jnp.concatenate([recv[first].astype(F32), recv[first + 1].astype(F32)], axis=0))
            for b, part in enumerate(swap_blocks(parts)):
                rows_ref[zh, pl.ds(32 * pair + b, 8, stride=4), :] = part
        for zl in range(3):
            rows_ref[zh, 16 * zl + HALF : 16 * zl + 16, :] = rows_ref[zh, 48 + 4 * zl : 52 + 4 * zl, :]

    def keep_block(recv, zh, ref):
        gather_block(recv, zh)
        ref[peer, zh] = rows_ref[zh, :48, :].astype(BF16).reshape(3, 16, LANES)

    def scatter_rows(tiles, send):
        for zh, tile in enumerate(tiles):
            rows_ref[zh, :48, :] = tile
            for zl in range(3):
                rows_ref[zh, 48 + 4 * zl : 52 + 4 * zl, :] = rows_ref[zh, 16 * zl + HALF : 16 * zl + 16, :]
            for pair in range(2):
                parts = [rows_ref[zh, pl.ds(32 * pair + b, 8, stride=4), :] for b in range(4)]
                for x, part in enumerate(swap_blocks(parts)):
                    first = 16 * zh + 4 * x + 2 * pair
                    send[first] = part[:4].astype(BF16)
                    send[first + 1] = part[4:].astype(BF16)

    def tiles_of(array):
        return [tile_of(array, t) for t in range(array.shape[1] // LANES)]

    def rows_of(ref, g):
        return jnp.concatenate([ref[g, zh].reshape(48, LANES) for zh in range(4)], axis=1)

    def all_rows(ref):
        return jnp.concatenate(
            [
                jnp.concatenate([ref[:, zh, zl].reshape(128, LANES) for zl in range(3)], axis=0)
                for zh in range(4)
            ],
            axis=1,
        )

    pad_ref[...] = jnp.zeros_like(pad_ref)
    slots_ref[...] = jnp.zeros_like(slots_ref)
    loads[0].wait()
    values = padded_transpose(pair_ref)
    centre = values - jnp.mean(values, axis=0, keepdims=True)
    inv_std = lax.rsqrt(jnp.mean(centre * centre, axis=0, keepdims=True) + EPS)
    zhat = centre * inv_std
    normed = zhat.astype(BF16)
    loads[1].wait()
    w_rows = w_proj_ref[...].astype(F32).T.astype(BF16)
    projected = dot(w_rows[128:], normed)
    right_gate = jax.nn.sigmoid(projected[:64])
    right_value = projected[64:]
    to_slots(right_gate * right_value, send_a)

    pl.semaphore_wait(barrier, GROUP - 1 + PEERS - 1)
    exchange_split(0, send_a, recv_a, right_sem)

    projected = dot(w_rows[:128], normed)
    left_gate = jax.nn.sigmoid(projected[:64])
    left_value = projected[64:]
    to_slots(left_gate * left_value, send_b)
    exchange(1, send_b, recv_b)

    for load in loads[2:]:
        load.wait()
    w_gate_t = w_gate_ref[...].astype(F32).T.astype(BF16)
    ow_t = ow_ref[...].astype(F32).T.astype(BF16)
    upstream = padded_transpose(d_out_ref)
    gate = jax.nn.sigmoid(dot(w_gate_t, normed))
    d_xhat = dot(ow_ref[...], (upstream * gate).astype(BF16))
    d_xhat_mean = jnp.mean(d_xhat, axis=0, keepdims=True)
    gate_slope = upstream * gate * (1.0 - gate)

    wait_all(recv_a.at[pl.ds(0, 48)], right_sem.at[0])
    for zh in nearer:
        keep_block(recv_a, zh, right_ref)
    start_across(nearer, 0)
    wait_all(recv_a.at[pl.ds(0, 16)], right_sem.at[1])
    keep_block(recv_a, opposite, right_ref)
    start_across([opposite], 1)
    to_sibling(nearer, 0)
    wait_all(recv_b, recv_sem.at[1])
    for zh in range(4):
        keep_block(recv_b, zh, left_ref)
    to_sibling([opposite], 1)
    wait_sends(0, send_a)
    wait_sends(1, send_b)
    wait_all(right_ref.at[pl.ds(0, 4)], recv_sem.at[2])
    right = all_rows(right_ref)
    scatter_rows(open_gaps(tiles_of(dot_t(rows_of(left_ref, peer), right))), send_d)
    exchange(4, send_d, recv_d)
    share(3, lambda to: left_ref.at[peer], left_ref)
    wait_all(right_ref.at[pl.ds(0, 3)], send_sem.at[2])
    wait_all(right_ref.at[pl.ds(0, 4)], send_sem.at[9])
    wait_all(recv_d, recv_sem.at[4])

    x = from_slots(recv_d)
    x_centre = x - jnp.mean(x, axis=0, keepdims=True)
    x_inv = lax.rsqrt(jnp.mean(x_centre * x_centre, axis=0, keepdims=True) + EPS)
    xhat = x_centre * x_inv
    d_x = (d_xhat - d_xhat_mean - xhat * jnp.mean(d_xhat * xhat, axis=0, keepdims=True)) * x_inv
    to_slots(d_x, send_e)
    exchange_split(5, send_e, recv_e, d_x_sem)

    mixed = dot(ow_t, xhat.astype(BF16))
    d_gate = (mixed * gate_slope).astype(BF16)
    d_normed = dot(w_gate_ref[...], d_gate)
    wait_sends(3, left_ref)
    wait_sends(4, send_d)

    wait_all(recv_e.at[pl.ds(0, 48)], d_x_sem.at[0])
    for zh in nearer:
        gather_block(recv_e, zh)
    wait_all(recv_e.at[pl.ds(0, 16)], d_x_sem.at[1])
    gather_block(recv_e, opposite)
    d_x_rows = jnp.concatenate(close_gaps([rows_ref[zh, :48, :] for zh in range(4)]), axis=1)
    padded = jnp.concatenate([d_x_rows, jnp.zeros((80, CELLS), F32)], axis=0)
    d_x_cols = padded.T.astype(BF16).reshape(3, PEERS, 16, LANES)
    for to in range(PEERS):
        send_f[to] = d_x_cols[:, to]
    recv_f[peer] = send_f[peer]
    share(6, lambda to: send_f.at[to], recv_f)

    scatter_rows(tiles_of(dot(d_x_rows.astype(BF16), right)), send_g)
    exchange(7, send_g, recv_g)
    wait_sends(5, send_e)
    wait_all(left_ref.at[pl.ds(0, PEERS - 1)], recv_sem.at[3])
    wait_all(recv_f.at[pl.ds(0, PEERS - 1)], recv_sem.at[6])
    d_right = None
    for g in range(PEERS):
        term = dot(recv_f[g].reshape(48, LANES)[:, :48], rows_of(left_ref, g))
        d_right = term if d_right is None else d_right + term
    scatter_rows(tiles_of(d_right), send_h)
    exchange(8, send_h, recv_h)

    def back(grad, gates, vals, columns):
        d_vals = grad * gates
        d_gates = d_vals * vals * (1.0 - gates)
        return dot(columns, jnp.concatenate([d_gates.astype(BF16), d_vals.astype(BF16)], axis=0))

    wait_sends(6, send_f)
    wait_all(recv_g, recv_sem.at[7])
    d_normed += back(from_slots(recv_g), left_gate, left_value, w_proj_ref[:, :128])
    wait_sends(7, send_g)
    wait_all(recv_h, recv_sem.at[8])
    d_normed += back(from_slots(recv_h), right_gate, right_value, w_proj_ref[:, 128:])
    grad_mean = jnp.mean(d_normed, axis=0, keepdims=True)
    cross_mean = jnp.mean(d_normed * zhat, axis=0, keepdims=True)
    d_pair = ((d_normed - grad_mean - zhat * cross_mean) * inv_std).T
    for i in range(TILE_I):
        out_ref[i, :HALF, :] = d_pair[32 * i : 32 * i + HALF]
        out_ref[i, HALF:, :] = d_pair[32 * i + 16 : 32 * i + 16 + HALF]
    wait_sends(8, send_h)


def per_device(pair, d_out, w_proj, w_gate, output_weight):
    slots = pltpu.VMEM((GROUP, 4, LANES), BF16)
    rows = pltpu.VMEM((PEERS, 4, 3, 16, LANES), BF16)
    blocks = pltpu.VMEM((PEERS, 3, 16, LANES), BF16)
    args = (pair, d_out, w_proj, w_gate, output_weight)
    return pl.pallas_call(
        body,
        out_shape=jax.ShapeDtypeStruct(pair.shape, F32),
        in_specs=[pl.BlockSpec(memory_space=pltpu.HBM)] * 5,
        out_specs=pl.BlockSpec(memory_space=pltpu.VMEM),
        scratch_shapes=[
            *(pltpu.VMEM(a.shape, a.dtype) for a in args),
            pltpu.VMEM((CELLS, LANES), F32),
            pltpu.VMEM((GROUP * 4 + 8, LANES), F32),
            pltpu.VMEM((4, 72, LANES), F32),
            rows, rows,
            slots, slots,
            slots, slots,
            slots, slots,
            slots, slots,
            blocks, blocks,
            slots, slots,
            slots, slots,
            pltpu.SemaphoreType.DMA((5,)),
            pltpu.SemaphoreType.DMA((10,)),
            pltpu.SemaphoreType.DMA((9,)),
            pltpu.SemaphoreType.DMA((2,)),
            pltpu.SemaphoreType.DMA((2,)),
            pltpu.SemaphoreType.DMA((4, 2)),
        ],
        compiler_params=pltpu.CompilerParams(
            collective_id=0, has_side_effects=True, vmem_limit_bytes=48 * 1024 * 1024
        ),
    )(*(pltpu.with_memory_space_constraint(a, pltpu.HBM) for a in args))


def solution(mesh):
    return jax.shard_map(
        per_device,
        mesh=mesh,
        in_specs=(P("row", "col", None), P("row", "col", None), P(), P(), P()),
        out_specs=P("row", "col", None),
        check_vma=False,
    )
```

```python
import jax
import jax.numpy as jnp
from jax import lax
from jax.experimental import pallas as pl
from jax.experimental.pallas import tpu as pltpu
from jax.sharding import PartitionSpec as P

EPS = 1e-05
MESH = pl.DeviceIdType.MESH
F32 = jnp.float32
BF16 = jnp.bfloat16

LANES = 128
GROUP = 64
PEERS = 8
HALF = 12
TILE_I = 12
CELLS = 384
TILES = CELLS // LANES


def dot(a, b):
    return lax.dot_general(a, b, (((1,), (0,)), ((), ())), preferred_element_type=F32)


def dot_t(a, b):
    return lax.dot_general(a, b, (((1,), (1,)), ((), ())), preferred_element_type=F32)


def swap_blocks(parts):
    lane = lax.broadcasted_iota(jnp.int32, parts[0].shape, 1)
    low = lane < 64
    even = (lane // 32) % 2 == 0
    p0, p1, p2, p3 = parts
    t0 = jnp.where(low, p0, pltpu.roll(p2, 64, 1))
    t2 = jnp.where(low, pltpu.roll(p0, 64, 1), p2)
    t1 = jnp.where(low, p1, pltpu.roll(p3, 64, 1))
    t3 = jnp.where(low, pltpu.roll(p1, 64, 1), p3)
    u0 = jnp.where(even, t0, pltpu.roll(t1, 32, 1))
    u1 = jnp.where(even, pltpu.roll(t0, 96, 1), t1)
    u2 = jnp.where(even, t2, pltpu.roll(t3, 32, 1))
    u3 = jnp.where(even, pltpu.roll(t2, 96, 1), t3)
    return u0, u1, u2, u3


def close_gaps(tiles):
    place = lax.broadcasted_iota(jnp.int32, tiles[0].shape, 1) % 16
    return [
        jnp.where(place < HALF, tiles[t], pltpu.roll(tiles[3], HALF - 4 * t, 1)) for t in range(3)
    ]


def open_gaps(tiles):
    place = lax.broadcasted_iota(jnp.int32, tiles[0].shape, 1) % 16
    back = [pltpu.roll(tiles[t], LANES - HALF + 4 * t, 1) for t in range(3)]
    return list(tiles) + [jnp.where(place < 4, back[0], jnp.where(place < 8, back[1], back[2]))]


def body(
    pair_hbm, d_out_hbm, w_proj_hbm, w_gate_hbm, ow_hbm, out_ref,
    pair_ref, d_out_ref, w_proj_ref, w_gate_ref, ow_ref,
    pad_ref, slots_ref, rows_ref, left_ref, right_ref,
    send_a, recv_a, send_b, recv_b, send_d, recv_d, send_e, recv_e, send_f, recv_f, send_g, recv_g, send_h, recv_h,
    in_sem, send_sem, recv_sem, right_sem, d_x_sem, across_sem,
):
    r = lax.axis_index("row")
    c = lax.axis_index("col")
    peer = lax.rem(r, PEERS)
    x_me = lax.rem(c, 4)
    z_lo = r // PEERS
    z_hi = c // 4
    z_me = z_hi * 4 + z_lo
    slot = (c // 4) * 16 + x_me * 4 + z_lo
    order_x = [lax.rem(x_me + dx, 4) for dx in (2, 1, 3, 0)]
    barrier = pltpu.get_barrier_semaphore()

    def each_of_group(act):
        def plane(dz, columns):
            z = lax.rem(z_me + dz, 16)
            high = lax.div(z, 4)
            low = z - 4 * high
            row = low * PEERS + peer
            col = high * 4
            base = high * 16 + low
            for x in columns:
                act((row, col + x), base + 4 * x)

        def step(n, carry):
            away = lax.div(n + 1, 2)
            plane(8 + jnp.where(lax.rem(n, 2) == 1, away, -away), order_x)
            return carry

        lax.fori_loop(0, 15, step, 0)
        plane(0, order_x[:3])

    def each_peer(act):
        def step(d, carry):
            to = lax.rem(peer + d, PEERS)
            act((z_lo * PEERS + to, c), to)
            return carry

        lax.fori_loop(1, PEERS, step, 0)

    loads = [
        pltpu.make_async_copy(src, dst, in_sem.at[n])
        for n, (src, dst) in enumerate((
            (pair_hbm, pair_ref), (w_proj_hbm, w_proj_ref), (d_out_hbm, d_out_ref),
            (w_gate_hbm, w_gate_ref), (ow_hbm, ow_ref),
        ))
    ]
    for load in loads:
        load.start()

    def greet(device, _):
        pl.semaphore_signal(barrier, inc=1, device_id=device, device_id_type=MESH)

    each_of_group(greet)
    each_peer(greet)

    def wait_all(ref, sem):
        pltpu.make_async_copy(ref, ref, sem).wait()

    def exchange(phase, send, recv):
        def one(device, to):
            pltpu.make_async_remote_copy(
                src_ref=send.at[to], dst_ref=recv.at[slot],
                send_sem=send_sem.at[phase], recv_sem=recv_sem.at[phase],
                device_id=device, device_id_type=MESH,
            ).start()

        each_of_group(one)
        pltpu.make_async_copy(send.at[slot], recv.at[slot], recv_sem.at[phase]).start()

    def exchange_split(phase, send, recv, sem):
        def one(device, to):
            opposite = jnp.where(lax.rem(to // 16 + 4 - z_hi, 4) == 2, 1, 0)
            pltpu.make_async_remote_copy(
                src_ref=send.at[to], dst_ref=recv.at[slot],
                send_sem=send_sem.at[phase], recv_sem=sem.at[opposite],
                device_id=device, device_id_type=MESH,
            ).start()

        each_of_group(one)
        pltpu.make_async_copy(send.at[slot], recv.at[slot], sem.at[0]).start()

    def share(phase, src_of, recv):
        def one(device, to):
            pltpu.make_async_remote_copy(
                src_ref=src_of(to), dst_ref=recv.at[peer],
                send_sem=send_sem.at[phase], recv_sem=recv_sem.at[phase],
                device_id=device, device_id_type=MESH,
            ).start()

        each_peer(one)

    sibling = peer + 1 - 2 * lax.rem(peer, 2)
    nearer = [lax.rem(z_hi + away, 4) for away in (0, 1, 3)]
    opposite = lax.rem(z_hi + 2, 4)

    def move_right(block, zh, to, send, recv):
        pltpu.make_async_remote_copy(
            src_ref=right_ref.at[block, zh], dst_ref=right_ref.at[block, zh], send_sem=send, recv_sem=recv,
            device_id=(z_lo * PEERS + to, c), device_id_type=MESH,
        ).start()

    def start_across(parts, part):
        for d in (2, 1, 3):
            for zh in parts:
                move_right(peer, zh, lax.rem(peer + 2 * d, PEERS), send_sem.at[2], across_sem.at[d, part])
        for zh in parts:
            move_right(peer, zh, sibling, send_sem.at[9], recv_sem.at[2])

    def to_sibling(parts, part):
        for d in (1, 3, 2):
            block = lax.rem(peer + PEERS - 2 * d, PEERS)
            wait_all(right_ref.at[block, pl.ds(0, len(parts))], across_sem.at[d, part])
            for zh in parts:
                move_right(block, zh, sibling, send_sem.at[9], recv_sem.at[2])

    def wait_sends(phase, ref):
        wait_all(ref.at[pl.ds(0, ref.shape[0] - 1)], send_sem.at[phase])

    def padded_transpose(ref):
        for pair in range(TILE_I // 2):
            cells = ref[4 * HALF * pair : 4 * HALF * (pair + 1), :].astype(F32)
            for half in range(4):
                at = 64 * pair + 16 * half
                pad_ref[at : at + HALF, :] = cells[HALF * half : HALF * (half + 1)]
        return pad_ref[...].T

    def tile_of(array, t):
        return array[:, LANES * t : LANES * (t + 1)]

    def to_slots(array, send):
        for a in range(TILES):
            slots_ref[pl.ds(a, GROUP, stride=4), :] = tile_of(array, a)
        for n in range(GROUP):
            send[n] = slots_ref[4 * n : 4 * n + 4, :].astype(BF16)

    def from_slots(recv):
        for n in range(GROUP):
            slots_ref[4 * n : 4 * n + 4, :] = recv[n].astype(F32)
        return jnp.concatenate([slots_ref[pl.ds(a, GROUP, stride=4), :] for a in range(TILES)], axis=1)

    def gather_block(recv, zh):
        for pair in range(2):
            parts = []
            for x in range(4):
                first = 16 * zh + 4 * x + 2 * pair
                parts.append(jnp.concatenate([recv[first].astype(F32), recv[first + 1].astype(F32)], axis=0))
            for b, part in enumerate(swap_blocks(parts)):
                rows_ref[zh, pl.ds(32 * pair + b, 8, stride=4), :] = part
        for zl in range(3):
            rows_ref[zh, 16 * zl + HALF : 16 * zl + 16, :] = rows_ref[zh, 48 + 4 * zl : 52 + 4 * zl, :]

    def keep_block(recv, zh, ref):
        gather_block(recv, zh)
        ref[peer, zh] = rows_ref[zh, :48, :].astype(BF16).reshape(3, 16, LANES)

    def scatter_rows(tiles, send):
        for zh, tile in enumerate(tiles):
            rows_ref[zh, :48, :] = tile
            for zl in range(3):
                rows_ref[zh, 48 + 4 * zl : 52 + 4 * zl, :] = rows_ref[zh, 16 * zl + HALF : 16 * zl + 16, :]
            for pair in range(2):
                parts = [rows_ref[zh, pl.ds(32 * pair + b, 8, stride=4), :] for b in range(4)]
                for x, part in enumerate(swap_blocks(parts)):
                    first = 16 * zh + 4 * x + 2 * pair
                    send[first] = part[:4].astype(BF16)
                    send[first + 1] = part[4:].astype(BF16)

    def tiles_of(array):
        return [tile_of(array, t) for t in range(array.shape[1] // LANES)]

    def rows_of(ref, g):
        return jnp.concatenate([ref[g, zh].reshape(48, LANES) for zh in range(4)], axis=1)

    def all_rows(ref):
        return jnp.concatenate(
            [
                jnp.concatenate([ref[:, zh, zl].reshape(128, LANES) for zl in range(3)], axis=0)
                for zh in range(4)
            ],
            axis=1,
        )

    pad_ref[...] = jnp.zeros_like(pad_ref)
    slots_ref[...] = jnp.zeros_like(slots_ref)
    loads[0].wait()
    values = padded_transpose(pair_ref)
    centre = values - jnp.mean(values, axis=0, keepdims=True)
    inv_std = lax.rsqrt(jnp.mean(centre * centre, axis=0, keepdims=True) + EPS)
    zhat = centre * inv_std
    normed = zhat.astype(BF16)
    loads[1].wait()
    w_rows = w_proj_ref[...].astype(F32).T.astype(BF16)
    projected = dot(w_rows[128:], normed)
    right_gate = jax.nn.sigmoid(projected[:64])
    right_value = projected[64:]
    to_slots(right_gate * right_value, send_a)

    pl.semaphore_wait(barrier, GROUP - 1 + PEERS - 1)
    exchange_split(0, send_a, recv_a, right_sem)

    projected = dot(w_rows[:128], normed)
    left_gate = jax.nn.sigmoid(projected[:64])
    left_value = projected[64:]
    to_slots(left_gate * left_value, send_b)
    exchange(1, send_b, recv_b)

    for load in loads[2:]:
        load.wait()
    w_gate_t = w_gate_ref[...].astype(F32).T.astype(BF16)
    ow_t = ow_ref[...].astype(F32).T.astype(BF16)
    upstream = padded_transpose(d_out_ref)
    gate = jax.nn.sigmoid(dot(w_gate_t, normed))
    d_xhat = dot(ow_ref[...], (upstream * gate).astype(BF16))
    d_xhat_mean = jnp.mean(d_xhat, axis=0, keepdims=True)
    gate_slope = upstream * gate * (1.0 - gate)

    wait_all(recv_a.at[pl.ds(0, 48)], right_sem.at[0])
    for zh in nearer:
        keep_block(recv_a, zh, right_ref)
    start_across(nearer, 0)
    wait_all(recv_a.at[pl.ds(0, 16)], right_sem.at[1])
    keep_block(recv_a, opposite, right_ref)
    start_across([opposite], 1)
    to_sibling(nearer, 0)
    wait_all(recv_b, recv_sem.at[1])
    for zh in range(4):
        keep_block(recv_b, zh, left_ref)
    to_sibling([opposite], 1)
    wait_sends(0, send_a)
    wait_sends(1, send_b)
    wait_all(right_ref.at[pl.ds(0, 4)], recv_sem.at[2])
    right = all_rows(right_ref)
    scatter_rows(open_gaps(tiles_of(dot_t(rows_of(left_ref, peer), right))), send_d)
    exchange(4, send_d, recv_d)
    share(3, lambda to: left_ref.at[peer], left_ref)
    wait_all(right_ref.at[pl.ds(0, 3)], send_sem.at[2])
    wait_all(right_ref.at[pl.ds(0, 4)], send_sem.at[9])
    wait_all(recv_d, recv_sem.at[4])

    x = from_slots(recv_d)
    x_centre = x - jnp.mean(x, axis=0, keepdims=True)
    x_inv = lax.rsqrt(jnp.mean(x_centre * x_centre, axis=0, keepdims=True) + EPS)
    xhat = x_centre * x_inv
    d_x = (d_xhat - d_xhat_mean - xhat * jnp.mean(d_xhat * xhat, axis=0, keepdims=True)) * x_inv
    to_slots(d_x, send_e)
    exchange_split(5, send_e, recv_e, d_x_sem)

    mixed = dot(ow_t, xhat.astype(BF16))
    d_gate = (mixed * gate_slope).astype(BF16)
    d_normed = dot(w_gate_ref[...], d_gate)
    wait_sends(3, left_ref)
    wait_sends(4, send_d)

    wait_all(recv_e.at[pl.ds(0, 48)], d_x_sem.at[0])
    for zh in nearer:
        gather_block(recv_e, zh)
    wait_all(recv_e.at[pl.ds(0, 16)], d_x_sem.at[1])
    gather_block(recv_e, opposite)
    d_x_rows = jnp.concatenate(close_gaps([rows_ref[zh, :48, :] for zh in range(4)]), axis=1)
    padded = jnp.concatenate([d_x_rows, jnp.zeros((80, CELLS), F32)], axis=0)
    d_x_cols = padded.T.astype(BF16).reshape(3, PEERS, 16, LANES)
    for to in range(PEERS):
        send_f[to] = d_x_cols[:, to]
    recv_f[peer] = send_f[peer]
    share(6, lambda to: send_f.at[to], recv_f)

    scatter_rows(tiles_of(dot(d_x_rows.astype(BF16), right)), send_g)
    exchange(7, send_g, recv_g)
    wait_sends(5, send_e)
    wait_all(left_ref.at[pl.ds(0, PEERS - 1)], recv_sem.at[3])
    wait_all(recv_f.at[pl.ds(0, PEERS - 1)], recv_sem.at[6])
    d_right = None
    for g in range(PEERS):
        term = dot(recv_f[g].reshape(48, LANES)[:, :48], rows_of(left_ref, g))
        d_right = term if d_right is None else d_right + term
    scatter_rows(tiles_of(d_right), send_h)
    exchange(8, send_h, recv_h)

    def back(grad, gates, vals, columns):
        d_vals = grad * gates
        d_gates = d_vals * vals * (1.0 - gates)
        return dot(columns, jnp.concatenate([d_gates.astype(BF16), d_vals.astype(BF16)], axis=0))

    wait_sends(6, send_f)
    wait_all(recv_g, recv_sem.at[7])
    d_normed += back(from_slots(recv_g), left_gate, left_value, w_proj_ref[:, :128])
    wait_sends(7, send_g)
    wait_all(recv_h, recv_sem.at[8])
    d_normed += back(from_slots(recv_h), right_gate, right_value, w_proj_ref[:, 128:])
    grad_mean = jnp.mean(d_normed, axis=0, keepdims=True)
    cross_mean = jnp.mean(d_normed * zhat, axis=0, keepdims=True)
    d_pair = ((d_normed - grad_mean - zhat * cross_mean) * inv_std).T
    for i in range(TILE_I):
        out_ref[i, :HALF, :] = d_pair[32 * i : 32 * i + HALF]
        out_ref[i, HALF:, :] = d_pair[32 * i + 16 : 32 * i + 16 + HALF]
    wait_sends(8, send_h)


def per_device(pair, d_out, w_proj, w_gate, output_weight):
    slots = pltpu.VMEM((GROUP, 4, LANES), BF16)
    rows = pltpu.VMEM((PEERS, 4, 3, 16, LANES), BF16)
    blocks = pltpu.VMEM((PEERS, 3, 16, LANES), BF16)
    args = (pair.reshape(-1, LANES), d_out.reshape(-1, LANES), w_proj, w_gate, output_weight)
    return pl.pallas_call(
        body,
        out_shape=jax.ShapeDtypeStruct(pair.shape, F32),
        in_specs=[pl.BlockSpec(memory_space=pltpu.HBM)] * 5,
        out_specs=pl.BlockSpec(memory_space=pltpu.VMEM),
        scratch_shapes=[
            *(pltpu.VMEM(a.shape, a.dtype) for a in args),
            pltpu.VMEM((CELLS, LANES), F32),
            pltpu.VMEM((GROUP * 4 + 8, LANES), F32),
            pltpu.VMEM((4, 72, LANES), F32),
            rows, rows,
            slots, slots,
            slots, slots,
            slots, slots,
            slots, slots,
            blocks, blocks,
            slots, slots,
            slots, slots,
            pltpu.SemaphoreType.DMA((5,)),
            pltpu.SemaphoreType.DMA((10,)),
            pltpu.SemaphoreType.DMA((9,)),
            pltpu.SemaphoreType.DMA((2,)),
            pltpu.SemaphoreType.DMA((2,)),
            pltpu.SemaphoreType.DMA((4, 2)),
        ],
        compiler_params=pltpu.CompilerParams(
            collective_id=0, has_side_effects=True, vmem_limit_bytes=48 * 1024 * 1024
        ),
    )(*(pltpu.with_memory_space_constraint(a, pltpu.HBM) for a in args))


def solution(mesh):
    return jax.shard_map(
        per_device,
        mesh=mesh,
        in_specs=(P("row", "col", None), P("row", "col", None), P(), P(), P()),
        out_specs=P("row", "col", None),
        check_vma=False,
    )
```

```python
import jax
import jax.numpy as jnp
from jax import lax
from jax.experimental import pallas as pl
from jax.experimental.pallas import tpu as pltpu
from jax.sharding import PartitionSpec as P

EPS = 1e-05
MESH = pl.DeviceIdType.MESH
F32 = jnp.float32
BF16 = jnp.bfloat16

LANES = 128
GROUP = 64
PEERS = 8
HALF = 12
TILE_I = 12
CELLS = 384
TILES = CELLS // LANES


def dot(a, b):
    return lax.dot_general(a, b, (((1,), (0,)), ((), ())), preferred_element_type=F32)


def dot_t(a, b):
    return lax.dot_general(a, b, (((1,), (1,)), ((), ())), preferred_element_type=F32)


def swap_blocks(parts):
    lane = lax.broadcasted_iota(jnp.int32, parts[0].shape, 1)
    low = lane < 64
    even = (lane // 32) % 2 == 0
    p0, p1, p2, p3 = parts
    t0 = jnp.where(low, p0, pltpu.roll(p2, 64, 1))
    t2 = jnp.where(low, pltpu.roll(p0, 64, 1), p2)
    t1 = jnp.where(low, p1, pltpu.roll(p3, 64, 1))
    t3 = jnp.where(low, pltpu.roll(p1, 64, 1), p3)
    u0 = jnp.where(even, t0, pltpu.roll(t1, 32, 1))
    u1 = jnp.where(even, pltpu.roll(t0, 96, 1), t1)
    u2 = jnp.where(even, t2, pltpu.roll(t3, 32, 1))
    u3 = jnp.where(even, pltpu.roll(t2, 96, 1), t3)
    return u0, u1, u2, u3


def close_gaps(tiles):
    place = lax.broadcasted_iota(jnp.int32, tiles[0].shape, 1) % 16
    return [
        jnp.where(place < HALF, tiles[t], pltpu.roll(tiles[3], HALF - 4 * t, 1)) for t in range(3)
    ]


def open_gaps(tiles):
    place = lax.broadcasted_iota(jnp.int32, tiles[0].shape, 1) % 16
    back = [pltpu.roll(tiles[t], LANES - HALF + 4 * t, 1) for t in range(3)]
    return list(tiles) + [jnp.where(place < 4, back[0], jnp.where(place < 8, back[1], back[2]))]


def body(
    pair_hbm, d_out_hbm, w_proj_hbm, w_gate_hbm, ow_hbm, out_ref,
    pair_ref, d_out_ref, w_proj_ref, w_gate_ref, ow_ref,
    pad_ref, slots_ref, rows_ref, left_ref, right_ref,
    send_a, recv_a, send_b, recv_b, send_d, recv_d, send_e, recv_e, send_f, recv_f, send_g, recv_g, send_h, recv_h,
    in_sem, send_sem, recv_sem, right_sem, d_x_sem, across_sem,
):
    r = lax.axis_index("row")
    c = lax.axis_index("col")
    peer = lax.rem(r, PEERS)
    x_me = lax.rem(c, 4)
    z_lo = r // PEERS
    z_hi = c // 4
    z_me = z_hi * 4 + z_lo
    slot = (c // 4) * 16 + x_me * 4 + z_lo
    order_x = [lax.rem(x_me + dx, 4) for dx in (2, 1, 3, 0)]
    barrier = pltpu.get_barrier_semaphore()

    def each_of_group(act):
        def plane(dz, columns):
            z = lax.rem(z_me + dz, 16)
            high = lax.div(z, 4)
            low = z - 4 * high
            row = low * PEERS + peer
            col = high * 4
            base = high * 16 + low
            for x in columns:
                act((row, col + x), base + 4 * x)

        def step(n, carry):
            away = lax.div(n + 1, 2)
            plane(8 + jnp.where(lax.rem(n, 2) == 1, away, -away), order_x)
            return carry

        lax.fori_loop(0, 15, step, 0)
        plane(0, order_x[:3])

    def each_peer(act):
        other_core = 1 - 2 * lax.rem(peer, 2)
        for dy in (2, 1, 3):
            to = lax.rem(peer + 2 * dy, PEERS)
            for peer_to in (to, to + other_core):
                act((z_lo * PEERS + peer_to, c), peer_to)
        act((z_lo * PEERS + peer + other_core, c), peer + other_core)

    loads = [
        pltpu.make_async_copy(src, dst, in_sem.at[n])
        for n, (src, dst) in enumerate((
            (pair_hbm, pair_ref), (w_proj_hbm, w_proj_ref), (d_out_hbm, d_out_ref),
            (w_gate_hbm, w_gate_ref), (ow_hbm, ow_ref),
        ))
    ]
    for load in loads:
        load.start()

    def greet(device, _):
        pl.semaphore_signal(barrier, inc=1, device_id=device, device_id_type=MESH)

    each_of_group(greet)
    each_peer(greet)

    def wait_all(ref, sem):
        pltpu.make_async_copy(ref, ref, sem).wait()

    def exchange(phase, send, recv):
        def one(device, to):
            pltpu.make_async_remote_copy(
                src_ref=send.at[to], dst_ref=recv.at[slot],
                send_sem=send_sem.at[phase], recv_sem=recv_sem.at[phase],
                device_id=device, device_id_type=MESH,
            ).start()

        each_of_group(one)
        pltpu.make_async_copy(send.at[slot], recv.at[slot], recv_sem.at[phase]).start()

    def exchange_split(phase, send, recv, sem):
        def one(device, to):
            opposite = jnp.where(lax.rem(to // 16 + 4 - z_hi, 4) == 2, 1, 0)
            pltpu.make_async_remote_copy(
                src_ref=send.at[to], dst_ref=recv.at[slot],
                send_sem=send_sem.at[phase], recv_sem=sem.at[opposite],
                device_id=device, device_id_type=MESH,
            ).start()

        each_of_group(one)
        pltpu.make_async_copy(send.at[slot], recv.at[slot], sem.at[0]).start()

    def share(phase, src_of, recv):
        def one(device, to):
            pltpu.make_async_remote_copy(
                src_ref=src_of(to), dst_ref=recv.at[peer],
                send_sem=send_sem.at[phase], recv_sem=recv_sem.at[phase],
                device_id=device, device_id_type=MESH,
            ).start()

        each_peer(one)

    sibling = peer + 1 - 2 * lax.rem(peer, 2)
    nearer = [lax.rem(z_hi + away, 4) for away in (0, 1, 3)]
    opposite = lax.rem(z_hi + 2, 4)

    def move_right(block, zh, to, send, recv):
        pltpu.make_async_remote_copy(
            src_ref=right_ref.at[block, zh], dst_ref=right_ref.at[block, zh], send_sem=send, recv_sem=recv,
            device_id=(z_lo * PEERS + to, c), device_id_type=MESH,
        ).start()

    def start_across(parts, part):
        for d in (2, 1, 3):
            for zh in parts:
                move_right(peer, zh, lax.rem(peer + 2 * d, PEERS), send_sem.at[2], across_sem.at[d, part])
        for zh in parts:
            move_right(peer, zh, sibling, send_sem.at[9], recv_sem.at[2])

    def to_sibling(parts, part):
        for d in (1, 3, 2):
            block = lax.rem(peer + PEERS - 2 * d, PEERS)
            wait_all(right_ref.at[block, pl.ds(0, len(parts))], across_sem.at[d, part])
            for zh in parts:
                move_right(block, zh, sibling, send_sem.at[9], recv_sem.at[2])

    def wait_sends(phase, ref):
        wait_all(ref.at[pl.ds(0, ref.shape[0] - 1)], send_sem.at[phase])

    def padded_transpose(ref):
        for pair in range(TILE_I // 2):
            cells = ref[4 * HALF * pair : 4 * HALF * (pair + 1), :].astype(F32)
            for half in range(4):
                at = 64 * pair + 16 * half
                pad_ref[at : at + HALF, :] = cells[HALF * half : HALF * (half + 1)]
        return pad_ref[...].T

    def tile_of(array, t):
        return array[:, LANES * t : LANES * (t + 1)]

    def to_slots(array, send):
        for a in range(TILES):
            slots_ref[pl.ds(a, GROUP, stride=4), :] = tile_of(array, a)
        for n in range(GROUP):
            send[n] = slots_ref[4 * n : 4 * n + 4, :].astype(BF16)

    def from_slots(recv):
        for n in range(GROUP):
            slots_ref[4 * n : 4 * n + 4, :] = recv[n].astype(F32)
        return jnp.concatenate([slots_ref[pl.ds(a, GROUP, stride=4), :] for a in range(TILES)], axis=1)

    def gather_block(recv, zh):
        for pair in range(2):
            parts = []
            for x in range(4):
                first = 16 * zh + 4 * x + 2 * pair
                parts.append(jnp.concatenate([recv[first].astype(F32), recv[first + 1].astype(F32)], axis=0))
            for b, part in enumerate(swap_blocks(parts)):
                rows_ref[zh, pl.ds(32 * pair + b, 8, stride=4), :] = part
        for zl in range(3):
            rows_ref[zh, 16 * zl + HALF : 16 * zl + 16, :] = rows_ref[zh, 48 + 4 * zl : 52 + 4 * zl, :]

    def keep_block(recv, zh, ref):
        gather_block(recv, zh)
        ref[peer, zh] = rows_ref[zh, :48, :].astype(BF16).reshape(3, 16, LANES)

    def scatter_rows(tiles, send):
        for zh, tile in enumerate(tiles):
            rows_ref[zh, :48, :] = tile
            for zl in range(3):
                rows_ref[zh, 48 + 4 * zl : 52 + 4 * zl, :] = rows_ref[zh, 16 * zl + HALF : 16 * zl + 16, :]
            for pair in range(2):
                parts = [rows_ref[zh, pl.ds(32 * pair + b, 8, stride=4), :] for b in range(4)]
                for x, part in enumerate(swap_blocks(parts)):
                    first = 16 * zh + 4 * x + 2 * pair
                    send[first] = part[:4].astype(BF16)
                    send[first + 1] = part[4:].astype(BF16)

    def tiles_of(array):
        return [tile_of(array, t) for t in range(array.shape[1] // LANES)]

    def rows_of(ref, g):
        return jnp.concatenate([ref[g, zh].reshape(48, LANES) for zh in range(4)], axis=1)

    def all_rows(ref):
        return jnp.concatenate(
            [
                jnp.concatenate([ref[:, zh, zl].reshape(128, LANES) for zl in range(3)], axis=0)
                for zh in range(4)
            ],
            axis=1,
        )

    pad_ref[...] = jnp.zeros_like(pad_ref)
    slots_ref[...] = jnp.zeros_like(slots_ref)
    loads[0].wait()
    values = padded_transpose(pair_ref)
    centre = values - jnp.mean(values, axis=0, keepdims=True)
    inv_std = lax.rsqrt(jnp.mean(centre * centre, axis=0, keepdims=True) + EPS)
    zhat = centre * inv_std
    normed = zhat.astype(BF16)
    loads[1].wait()
    w_rows = w_proj_ref[...].astype(F32).T.astype(BF16)
    projected = dot(w_rows[128:], normed)
    right_gate = jax.nn.sigmoid(projected[:64])
    right_value = projected[64:]
    to_slots(right_gate * right_value, send_a)

    pl.semaphore_wait(barrier, GROUP - 1 + PEERS - 1)
    exchange_split(0, send_a, recv_a, right_sem)

    projected = dot(w_rows[:128], normed)
    left_gate = jax.nn.sigmoid(projected[:64])
    left_value = projected[64:]
    to_slots(left_gate * left_value, send_b)
    exchange(1, send_b, recv_b)

    for load in loads[2:]:
        load.wait()
    w_gate_t = w_gate_ref[...].astype(F32).T.astype(BF16)
    ow_t = ow_ref[...].astype(F32).T.astype(BF16)
    upstream = padded_transpose(d_out_ref)
    gate = jax.nn.sigmoid(dot(w_gate_t, normed))
    d_xhat = dot(ow_ref[...], (upstream * gate).astype(BF16))
    d_xhat_mean = jnp.mean(d_xhat, axis=0, keepdims=True)
    gate_slope = upstream * gate * (1.0 - gate)

    wait_all(recv_a.at[pl.ds(0, 48)], right_sem.at[0])
    for zh in nearer:
        keep_block(recv_a, zh, right_ref)
    start_across(nearer, 0)
    wait_all(recv_a.at[pl.ds(0, 16)], right_sem.at[1])
    keep_block(recv_a, opposite, right_ref)
    start_across([opposite], 1)
    to_sibling(nearer, 0)
    wait_all(recv_b, recv_sem.at[1])
    for zh in range(4):
        keep_block(recv_b, zh, left_ref)
    to_sibling([opposite], 1)
    wait_sends(0, send_a)
    wait_sends(1, send_b)
    wait_all(right_ref.at[pl.ds(0, 4)], recv_sem.at[2])
    right = all_rows(right_ref)
    scatter_rows(open_gaps(tiles_of(dot_t(rows_of(left_ref, peer), right))), send_d)
    exchange(4, send_d, recv_d)
    share(3, lambda to: left_ref.at[peer], left_ref)
    wait_all(right_ref.at[pl.ds(0, 3)], send_sem.at[2])
    wait_all(right_ref.at[pl.ds(0, 4)], send_sem.at[9])
    wait_all(recv_d, recv_sem.at[4])

    x = from_slots(recv_d)
    x_centre = x - jnp.mean(x, axis=0, keepdims=True)
    x_inv = lax.rsqrt(jnp.mean(x_centre * x_centre, axis=0, keepdims=True) + EPS)
    xhat = x_centre * x_inv
    d_x = (d_xhat - d_xhat_mean - xhat * jnp.mean(d_xhat * xhat, axis=0, keepdims=True)) * x_inv
    to_slots(d_x, send_e)
    exchange_split(5, send_e, recv_e, d_x_sem)

    mixed = dot(ow_t, xhat.astype(BF16))
    d_gate = (mixed * gate_slope).astype(BF16)
    d_normed = dot(w_gate_ref[...], d_gate)
    wait_sends(3, left_ref)
    wait_sends(4, send_d)

    wait_all(recv_e.at[pl.ds(0, 48)], d_x_sem.at[0])
    for zh in nearer:
        gather_block(recv_e, zh)
    wait_all(recv_e.at[pl.ds(0, 16)], d_x_sem.at[1])
    gather_block(recv_e, opposite)
    d_x_rows = jnp.concatenate(close_gaps([rows_ref[zh, :48, :] for zh in range(4)]), axis=1)
    padded = jnp.concatenate([d_x_rows, jnp.zeros((80, CELLS), F32)], axis=0)
    d_x_cols = padded.T.astype(BF16).reshape(3, PEERS, 16, LANES)
    for to in range(PEERS):
        send_f[to] = d_x_cols[:, to]
    recv_f[peer] = send_f[peer]
    share(6, lambda to: send_f.at[to], recv_f)

    scatter_rows(tiles_of(dot(d_x_rows.astype(BF16), right)), send_g)
    exchange(7, send_g, recv_g)
    wait_sends(5, send_e)
    wait_all(left_ref.at[pl.ds(0, PEERS - 1)], recv_sem.at[3])
    wait_all(recv_f.at[pl.ds(0, PEERS - 1)], recv_sem.at[6])
    d_right = None
    for g in range(PEERS):
        term = dot(recv_f[g].reshape(48, LANES)[:, :48], rows_of(left_ref, g))
        d_right = term if d_right is None else d_right + term
    scatter_rows(tiles_of(d_right), send_h)
    exchange(8, send_h, recv_h)

    def back(grad, gates, vals, columns):
        d_vals = grad * gates
        d_gates = d_vals * vals * (1.0 - gates)
        return dot(columns, jnp.concatenate([d_gates.astype(BF16), d_vals.astype(BF16)], axis=0))

    wait_sends(6, send_f)
    wait_all(recv_g, recv_sem.at[7])
    d_normed += back(from_slots(recv_g), left_gate, left_value, w_proj_ref[:, :128])
    wait_sends(7, send_g)
    wait_all(recv_h, recv_sem.at[8])
    d_normed += back(from_slots(recv_h), right_gate, right_value, w_proj_ref[:, 128:])
    grad_mean = jnp.mean(d_normed, axis=0, keepdims=True)
    cross_mean = jnp.mean(d_normed * zhat, axis=0, keepdims=True)
    d_pair = ((d_normed - grad_mean - zhat * cross_mean) * inv_std).T
    for i in range(TILE_I):
        out_ref[i, :HALF, :] = d_pair[32 * i : 32 * i + HALF]
        out_ref[i, HALF:, :] = d_pair[32 * i + 16 : 32 * i + 16 + HALF]
    wait_sends(8, send_h)


def per_device(pair, d_out, w_proj, w_gate, output_weight):
    slots = pltpu.VMEM((GROUP, 4, LANES), BF16)
    rows = pltpu.VMEM((PEERS, 4, 3, 16, LANES), BF16)
    blocks = pltpu.VMEM((PEERS, 3, 16, LANES), BF16)
    args = (pair.reshape(-1, LANES), d_out.reshape(-1, LANES), w_proj, w_gate, output_weight)
    return pl.pallas_call(
        body,
        out_shape=jax.ShapeDtypeStruct(pair.shape, F32),
        in_specs=[pl.BlockSpec(memory_space=pltpu.HBM)] * 5,
        out_specs=pl.BlockSpec(memory_space=pltpu.VMEM),
        scratch_shapes=[
            *(pltpu.VMEM(a.shape, a.dtype) for a in args),
            pltpu.VMEM((CELLS, LANES), F32),
            pltpu.VMEM((GROUP * 4 + 8, LANES), F32),
            pltpu.VMEM((4, 72, LANES), F32),
            rows, rows,
            slots, slots,
            slots, slots,
            slots, slots,
            slots, slots,
            blocks, blocks,
            slots, slots,
            slots, slots,
            pltpu.SemaphoreType.DMA((5,)),
            pltpu.SemaphoreType.DMA((10,)),
            pltpu.SemaphoreType.DMA((9,)),
            pltpu.SemaphoreType.DMA((2,)),
            pltpu.SemaphoreType.DMA((2,)),
            pltpu.SemaphoreType.DMA((4, 2)),
        ],
        compiler_params=pltpu.CompilerParams(
            collective_id=0, has_side_effects=True, vmem_limit_bytes=48 * 1024 * 1024
        ),
    )(*(pltpu.with_memory_space_constraint(a, pltpu.HBM) for a in args))


def solution(mesh):
    return jax.shard_map(
        per_device,
        mesh=mesh,
        in_specs=(P("row", "col", None), P("row", "col", None), P(), P(), P()),
        out_specs=P("row", "col", None),
        check_vma=False,
    )
```

```python
import jax
import jax.numpy as jnp
from jax import lax
from jax.experimental import pallas as pl
from jax.experimental.pallas import tpu as pltpu
from jax.sharding import PartitionSpec as P

EPS = 1e-05
MESH = pl.DeviceIdType.MESH
F32 = jnp.float32
BF16 = jnp.bfloat16

LANES = 128
GROUP = 64
PEERS = 8
HALF = 12
TILE_I = 12
CELLS = 384
TILES = CELLS // LANES


def dot(a, b):
    return lax.dot_general(a, b, (((1,), (0,)), ((), ())), preferred_element_type=F32)


def dot_t(a, b):
    return lax.dot_general(a, b, (((1,), (1,)), ((), ())), preferred_element_type=F32)


def swap_blocks(parts):
    lane = lax.broadcasted_iota(jnp.int32, parts[0].shape, 1)
    low = lane < 64
    even = (lane // 32) % 2 == 0
    p0, p1, p2, p3 = parts
    t0 = jnp.where(low, p0, pltpu.roll(p2, 64, 1))
    t2 = jnp.where(low, pltpu.roll(p0, 64, 1), p2)
    t1 = jnp.where(low, p1, pltpu.roll(p3, 64, 1))
    t3 = jnp.where(low, pltpu.roll(p1, 64, 1), p3)
    u0 = jnp.where(even, t0, pltpu.roll(t1, 32, 1))
    u1 = jnp.where(even, pltpu.roll(t0, 96, 1), t1)
    u2 = jnp.where(even, t2, pltpu.roll(t3, 32, 1))
    u3 = jnp.where(even, pltpu.roll(t2, 96, 1), t3)
    return u0, u1, u2, u3


def close_gaps(tiles):
    place = lax.broadcasted_iota(jnp.int32, tiles[0].shape, 1) % 16
    return [
        jnp.where(place < HALF, tiles[t], pltpu.roll(tiles[3], HALF - 4 * t, 1)) for t in range(3)
    ]


def open_gaps(tiles):
    place = lax.broadcasted_iota(jnp.int32, tiles[0].shape, 1) % 16
    back = [pltpu.roll(tiles[t], LANES - HALF + 4 * t, 1) for t in range(3)]
    return list(tiles) + [jnp.where(place < 4, back[0], jnp.where(place < 8, back[1], back[2]))]


def body(
    pair_hbm, d_out_hbm, w_proj_hbm, w_gate_hbm, ow_hbm, out_ref,
    pair_ref, d_out_ref, w_proj_ref, w_gate_ref, ow_ref,
    pad_ref, slots_ref, rows_ref, left_ref, right_ref,
    send_a, recv_a, send_b, recv_b, send_d, recv_d, send_e, recv_e, send_f, recv_f, send_g, recv_g, send_h, recv_h,
    in_sem, send_sem, recv_sem, right_sem, d_x_sem, across_sem,
):
    r = lax.axis_index("row")
    c = lax.axis_index("col")
    peer = lax.rem(r, PEERS)
    x_me = lax.rem(c, 4)
    z_lo = r // PEERS
    z_hi = c // 4
    z_me = z_hi * 4 + z_lo
    slot = (c // 4) * 16 + x_me * 4 + z_lo
    order_x = [lax.rem(x_me + dx, 4) for dx in (2, 1, 3, 0)]
    barrier = pltpu.get_barrier_semaphore()

    def each_of_group(act):
        def plane(dz, columns):
            z = lax.rem(z_me + dz, 16)
            high = lax.div(z, 4)
            low = z - 4 * high
            row = low * PEERS + peer
            col = high * 4
            base = high * 16 + low
            for x in columns:
                act((row, col + x), base + 4 * x)

        def step(n, carry):
            away = lax.div(n + 1, 2)
            plane(8 + jnp.where(lax.rem(n, 2) == 1, away, -away), order_x)
            return carry

        lax.fori_loop(0, 15, step, 0)
        plane(0, order_x[:3])

    def each_peer(act):
        other_core = 1 - 2 * lax.rem(peer, 2)
        for dy in (2, 1, 3):
            to = lax.rem(peer + 2 * dy, PEERS)
            for peer_to in (to, to + other_core):
                act((z_lo * PEERS + peer_to, c), peer_to)
        act((z_lo * PEERS + peer + other_core, c), peer + other_core)

    loads = [
        pltpu.make_async_copy(src, dst, in_sem.at[n])
        for n, (src, dst) in enumerate((
            (pair_hbm, pair_ref), (w_proj_hbm, w_proj_ref), (d_out_hbm, d_out_ref),
            (w_gate_hbm, w_gate_ref), (ow_hbm, ow_ref),
        ))
    ]
    for load in loads:
        load.start()

    def greet(device, _):
        pl.semaphore_signal(barrier, inc=1, device_id=device, device_id_type=MESH)

    each_of_group(greet)
    each_peer(greet)

    def wait_all(ref, sem):
        pltpu.make_async_copy(ref, ref, sem).wait()

    def exchange(phase, send, recv):
        def one(device, to):
            pltpu.make_async_remote_copy(
                src_ref=send.at[to], dst_ref=recv.at[slot],
                send_sem=send_sem.at[phase], recv_sem=recv_sem.at[phase],
                device_id=device, device_id_type=MESH,
            ).start()

        each_of_group(one)
        pltpu.make_async_copy(send.at[slot], recv.at[slot], recv_sem.at[phase]).start()

    def exchange_split(phase, send, recv, sem):
        def one(device, to):
            opposite = jnp.where(lax.rem(to // 16 + 4 - z_hi, 4) == 2, 1, 0)
            pltpu.make_async_remote_copy(
                src_ref=send.at[to], dst_ref=recv.at[slot],
                send_sem=send_sem.at[phase], recv_sem=sem.at[opposite],
                device_id=device, device_id_type=MESH,
            ).start()

        each_of_group(one)
        pltpu.make_async_copy(send.at[slot], recv.at[slot], sem.at[0]).start()

    def share(phase, src_of, recv):
        def one(device, to):
            pltpu.make_async_remote_copy(
                src_ref=src_of(to), dst_ref=recv.at[peer],
                send_sem=send_sem.at[phase], recv_sem=recv_sem.at[phase],
                device_id=device, device_id_type=MESH,
            ).start()

        each_peer(one)

    sibling = peer + 1 - 2 * lax.rem(peer, 2)
    nearer = [lax.rem(z_hi + away, 4) for away in (0, 1, 3)]
    opposite = lax.rem(z_hi + 2, 4)

    def move_right(block, zh, to, send, recv):
        pltpu.make_async_remote_copy(
            src_ref=right_ref.at[block, zh], dst_ref=right_ref.at[block, zh], send_sem=send, recv_sem=recv,
            device_id=(z_lo * PEERS + to, c), device_id_type=MESH,
        ).start()

    def start_across(parts, part):
        for d in (2, 1, 3):
            for zh in parts:
                move_right(peer, zh, lax.rem(peer + 2 * d, PEERS), send_sem.at[2], across_sem.at[d, part])
        for zh in parts:
            move_right(peer, zh, sibling, send_sem.at[9], recv_sem.at[2])

    def to_sibling(parts, part):
        for d in (1, 3, 2):
            block = lax.rem(peer + PEERS - 2 * d, PEERS)
            wait_all(right_ref.at[block, pl.ds(0, len(parts))], across_sem.at[d, part])
            for zh in parts:
                move_right(block, zh, sibling, send_sem.at[9], recv_sem.at[2])

    def wait_sends(phase, ref):
        wait_all(ref.at[pl.ds(0, ref.shape[0] - 1)], send_sem.at[phase])

    def padded_transpose(ref):
        for pair in range(TILE_I // 2):
            cells = ref[4 * HALF * pair : 4 * HALF * (pair + 1), :].astype(F32)
            for half in range(4):
                at = 64 * pair + 16 * half
                pad_ref[at : at + HALF, :] = cells[HALF * half : HALF * (half + 1)]
        return pad_ref[...].T

    def tile_of(array, t):
        return array[:, LANES * t : LANES * (t + 1)]

    def to_slots(array, send):
        for a in range(TILES):
            slots_ref[pl.ds(a, GROUP, stride=4), :] = tile_of(array, a)
        for n in range(GROUP):
            send[n] = slots_ref[4 * n : 4 * n + 4, :].astype(BF16)

    def from_slots(recv):
        for n in range(GROUP):
            slots_ref[4 * n : 4 * n + 4, :] = recv[n].astype(F32)
        return jnp.concatenate([slots_ref[pl.ds(a, GROUP, stride=4), :] for a in range(TILES)], axis=1)

    def gather_block(recv, zh):
        for pair in range(2):
            parts = []
            for x in range(4):
                first = 16 * zh + 4 * x + 2 * pair
                parts.append(jnp.concatenate([recv[first].astype(F32), recv[first + 1].astype(F32)], axis=0))
            for b, part in enumerate(swap_blocks(parts)):
                rows_ref[zh, pl.ds(32 * pair + b, 8, stride=4), :] = part
        for zl in range(3):
            rows_ref[zh, 16 * zl + HALF : 16 * zl + 16, :] = rows_ref[zh, 48 + 4 * zl : 52 + 4 * zl, :]

    def keep_block(recv, zh, ref):
        gather_block(recv, zh)
        ref[peer, zh] = rows_ref[zh, :48, :].astype(BF16).reshape(3, 16, LANES)

    def scatter_rows(tiles, send):
        for zh, tile in enumerate(tiles):
            rows_ref[zh, :48, :] = tile
            for zl in range(3):
                rows_ref[zh, 48 + 4 * zl : 52 + 4 * zl, :] = rows_ref[zh, 16 * zl + HALF : 16 * zl + 16, :]
            for pair in range(2):
                parts = [rows_ref[zh, pl.ds(32 * pair + b, 8, stride=4), :] for b in range(4)]
                for x, part in enumerate(swap_blocks(parts)):
                    first = 16 * zh + 4 * x + 2 * pair
                    send[first] = part[:4].astype(BF16)
                    send[first + 1] = part[4:].astype(BF16)

    def tiles_of(array):
        return [tile_of(array, t) for t in range(array.shape[1] // LANES)]

    def rows_of(ref, g):
        return jnp.concatenate([ref[g, zh].reshape(48, LANES) for zh in range(4)], axis=1)

    def all_rows(ref):
        return jnp.concatenate(
            [
                jnp.concatenate([ref[:, zh, zl].reshape(128, LANES) for zl in range(3)], axis=0)
                for zh in range(4)
            ],
            axis=1,
        )

    pad_ref[...] = jnp.zeros_like(pad_ref)
    slots_ref[...] = jnp.zeros_like(slots_ref)
    loads[0].wait()
    values = padded_transpose(pair_ref)
    centre = values - jnp.mean(values, axis=0, keepdims=True)
    inv_std = lax.rsqrt(jnp.mean(centre * centre, axis=0, keepdims=True) + EPS)
    zhat = centre * inv_std
    normed = zhat.astype(BF16)
    loads[1].wait()
    w_rows = w_proj_ref[...].astype(F32).T.astype(BF16)
    projected = dot(w_rows[128:], normed)
    right_gate = jax.nn.sigmoid(projected[:64])
    right_value = projected[64:]
    to_slots(right_gate * right_value, send_a)

    pl.semaphore_wait(barrier, GROUP - 1 + PEERS - 1)
    exchange_split(0, send_a, recv_a, right_sem)

    projected = dot(w_rows[:128], normed)
    left_gate = jax.nn.sigmoid(projected[:64])
    left_value = projected[64:]
    to_slots(left_gate * left_value, send_b)
    exchange(1, send_b, recv_b)

    for load in loads[2:]:
        load.wait()
    w_gate_t = w_gate_ref[...].astype(F32).T.astype(BF16)
    ow_t = ow_ref[...].astype(F32).T.astype(BF16)
    upstream = padded_transpose(d_out_ref)
    gate = jax.nn.sigmoid(dot(w_gate_t, normed))
    d_xhat = dot(ow_ref[...], (upstream * gate).astype(BF16))
    d_xhat_mean = jnp.mean(d_xhat, axis=0, keepdims=True)
    gate_slope = upstream * gate * (1.0 - gate)

    wait_all(recv_a.at[pl.ds(0, 48)], right_sem.at[0])
    for zh in nearer:
        keep_block(recv_a, zh, right_ref)
    start_across(nearer, 0)
    wait_all(recv_a.at[pl.ds(0, 16)], right_sem.at[1])
    keep_block(recv_a, opposite, right_ref)
    start_across([opposite], 1)
    to_sibling(nearer, 0)
    wait_all(recv_b, recv_sem.at[1])
    for zh in range(4):
        keep_block(recv_b, zh, left_ref)
    to_sibling([opposite], 1)
    wait_sends(0, send_a)
    wait_sends(1, send_b)
    wait_all(right_ref.at[pl.ds(0, 4)], recv_sem.at[2])
    right = all_rows(right_ref)
    scatter_rows(open_gaps(tiles_of(dot_t(rows_of(left_ref, peer), right))), send_d)
    exchange(4, send_d, recv_d)
    share(3, lambda to: left_ref.at[peer], left_ref)
    wait_all(right_ref.at[pl.ds(0, 3)], send_sem.at[2])
    wait_all(right_ref.at[pl.ds(0, 4)], send_sem.at[9])
    wait_all(recv_d, recv_sem.at[4])

    x = from_slots(recv_d)
    x_centre = x - jnp.mean(x, axis=0, keepdims=True)
    x_inv = lax.rsqrt(jnp.mean(x_centre * x_centre, axis=0, keepdims=True) + EPS)
    xhat = x_centre * x_inv
    d_x = (d_xhat - d_xhat_mean - xhat * jnp.mean(d_xhat * xhat, axis=0, keepdims=True)) * x_inv
    to_slots(d_x, send_e)
    exchange_split(5, send_e, recv_e, d_x_sem)

    mixed = dot(ow_t, xhat.astype(BF16))
    d_gate = (mixed * gate_slope).astype(BF16)
    d_normed = dot(w_gate_ref[...], d_gate)
    wait_sends(3, left_ref)
    wait_sends(4, send_d)

    wait_all(recv_e.at[pl.ds(0, 48)], d_x_sem.at[0])
    for zh in nearer:
        gather_block(recv_e, zh)
    wait_all(recv_e.at[pl.ds(0, 16)], d_x_sem.at[1])
    gather_block(recv_e, opposite)
    d_x_rows = jnp.concatenate(close_gaps([rows_ref[zh, :48, :] for zh in range(4)]), axis=1)
    padded = jnp.concatenate([d_x_rows, jnp.zeros((80, CELLS), F32)], axis=0)
    d_x_cols = padded.T.astype(BF16).reshape(3, PEERS, 16, LANES)
    for to in range(PEERS):
        send_f[to] = d_x_cols[:, to]
    recv_f[peer] = send_f[peer]
    share(6, lambda to: send_f.at[to], recv_f)

    scatter_rows(tiles_of(dot(d_x_rows.astype(BF16), right)), send_g)
    exchange(7, send_g, recv_g)
    wait_sends(5, send_e)
    wait_all(left_ref.at[pl.ds(0, PEERS - 1)], recv_sem.at[3])
    wait_all(recv_f.at[pl.ds(0, PEERS - 1)], recv_sem.at[6])
    d_right = None
    for g in range(PEERS):
        term = dot(recv_f[g].reshape(48, LANES)[:, :48], rows_of(left_ref, g))
        d_right = term if d_right is None else d_right + term
    scatter_rows(tiles_of(d_right), send_h)
    exchange(8, send_h, recv_h)

    def back(grad, gates, vals, columns):
        d_vals = grad * gates
        d_gates = d_vals * vals * (1.0 - gates)
        return dot(columns, jnp.concatenate([d_gates.astype(BF16), d_vals.astype(BF16)], axis=0))

    wait_sends(6, send_f)
    wait_all(recv_g, recv_sem.at[7])
    d_normed += back(from_slots(recv_g), left_gate, left_value, w_proj_ref[:, :128])
    wait_sends(7, send_g)
    wait_all(recv_h, recv_sem.at[8])
    d_normed += back(from_slots(recv_h), right_gate, right_value, w_proj_ref[:, 128:])
    grad_mean = jnp.mean(d_normed, axis=0, keepdims=True)
    cross_mean = jnp.mean(d_normed * zhat, axis=0, keepdims=True)
    d_pair = ((d_normed - grad_mean - zhat * cross_mean) * inv_std).T
    for i in range(TILE_I):
        out_ref[i, :HALF, :] = d_pair[32 * i : 32 * i + HALF]
        out_ref[i, HALF:, :] = d_pair[32 * i + 16 : 32 * i + 16 + HALF]
    wait_sends(8, send_h)


def per_device(pair, d_out, w_proj, w_gate, output_weight):
    slots = pltpu.VMEM((GROUP, 4, LANES), BF16)
    rows = pltpu.VMEM((PEERS, 4, 3, 16, LANES), BF16)
    blocks = pltpu.VMEM((PEERS, 3, 16, LANES), BF16)
    args = (pair.reshape(-1, LANES), d_out.reshape(-1, LANES), w_proj, w_gate, output_weight)
    return pl.pallas_call(
        body,
        out_shape=jax.ShapeDtypeStruct(pair.shape, F32),
        in_specs=[pl.BlockSpec(memory_space=pltpu.HBM)] * 5,
        out_specs=pl.BlockSpec(memory_space=pltpu.VMEM),
        scratch_shapes=[
            *(pltpu.VMEM(a.shape, a.dtype) for a in args),
            pltpu.VMEM((CELLS, LANES), F32),
            pltpu.VMEM((GROUP * 4 + 8, LANES), F32),
            pltpu.VMEM((4, 72, LANES), F32),
            rows, rows,
            slots, slots,
            slots, slots,
            slots, slots,
            slots, slots,
            blocks, blocks,
            slots, slots,
            slots, slots,
            pltpu.SemaphoreType.DMA((5,)),
            pltpu.SemaphoreType.DMA((10,)),
            pltpu.SemaphoreType.DMA((9,)),
            pltpu.SemaphoreType.DMA((2,)),
            pltpu.SemaphoreType.DMA((2,)),
            pltpu.SemaphoreType.DMA((4, 2)),
        ],
        compiler_params=pltpu.CompilerParams(
            collective_id=0, has_side_effects=True, skip_device_barrier=True, vmem_limit_bytes=48 * 1024 * 1024
        ),
    )(*(pltpu.with_memory_space_constraint(a, pltpu.HBM) for a in args))


def solution(mesh):
    return jax.shard_map(
        per_device,
        mesh=mesh,
        in_specs=(P("row", "col", None), P("row", "col", None), P(), P(), P()),
        out_specs=P("row", "col", None),
        check_vma=False,
    )
```
